128 devices in a mesh: ctx: 32 (over z_lo, y, x), tok: 4 (over z_hi, core).
Axes of the slice: x: 4, y: 4, z: 4 (z_hi: 2, z_lo: 2; z = z_hi * 2 + z_lo), core: 2. Of those that a mesh axis runs over, the one named last changes fastest.
Arguments:
- frames: bfloat16 [65536, 512], P('ctx'), may hold values from -128 to 128
- tokens: bfloat16 [8192, 512], P('tok'), may hold values from -12 to 12
- frame_mass: float32 [65536], P('ctx'), may hold values from 0.25 to 12
- token_mass: float32 [8192], P('tok'), may hold values from 0.25 to 12
Outputs:
- frame_map: bfloat16 [65536, 512], P('ctx')
- token_map: bfloat16 [8192, 512], P('tok')
- mass_ratio: float32 [65536], P('ctx')
The draws below stay inside these ranges and needn't reach their ends.
All inputs are finite; a program needn't handle non-finite values.
Results may differ from the reference program's by a relative error of at most 0.0047.
Values may be sent and summed in bfloat16 or wider, within the bound.
No kernel may reach another device: no remote copies, remote signals or barrier semaphores. Data moves between devices by JAX's collectives and lax.ppermute only.
A program may use at most 128 MiB of HBM per device.

```python
import math
import jax
import jax.numpy as jnp
from jax import lax

D = 512
F_DEV = 2048
NT = 8192
ITERS = 2
NF = 65536


def anchor_rows(key):
    return jnp.clip(jax.random.normal(jax.random.fold_in(key, 77), (3, D), jnp.float32), -3.0, 3.0)


def anchor_noise(key):
    return jnp.clip(jax.random.normal(jax.random.fold_in(key, 79), (3, D), jnp.float32), -3.0, 3.0)


def frame_strengths():
    targets = jnp.array([110.0, 220.0, 330.0], jnp.float32)[:, None]
    return targets / (3.0 * math.sqrt(D))


def draw_tokens(key, part):
    anchors = anchor_rows(key)
    noise = anchor_noise(key)
    key = jax.random.fold_in(key, 11)
    first_key, second_key = jax.random.split(key, 2)
    base = jnp.clip(jax.random.normal(first_key, (NT, D), jnp.float32), -6.0, 6.0)
    scales = jnp.exp(jax.random.uniform(second_key, (NT, 1), jnp.float32, math.log(0.5), math.log(1.5)))
    result = base * scales
    spread = 2.0 / (3.0 * frame_strengths() * 3.0)
    places = jnp.array([NT // 7, 3 * NT // 7, 5 * NT // 7], jnp.int32)
    result = result.at[places].set(3.0 * anchors)
    result = result.at[places + 1].set(3.0 * (anchors + spread * noise))
    return result.astype(jnp.bfloat16)


def draw_frames(key, part):
    anchors = anchor_rows(key)
    key = jax.random.fold_in(key, 13)
    first_key, second_key = jax.random.split(key, 2)
    base = jnp.clip(jax.random.normal(first_key, (NF, D), jnp.float32), -6.0, 6.0)
    scales = jnp.exp(jax.random.uniform(second_key, (NF, 1), jnp.float32, 0.0, math.log(10.0)))
    result = base * scales
    places = jnp.array([NF // 7, 3 * NF // 7, 5 * NF // 7], jnp.int32)
    result = result.at[places].set(frame_strengths() * anchors)
    return result.astype(jnp.bfloat16)


def rising_mass(key, count):
    position = jnp.arange(count).astype(jnp.float32)
    rising = 1.0 + 2.0 * position / (count - 1)
    base = jnp.exp(jax.random.uniform(key, (count,), jnp.float32, math.log(0.25), math.log(4.0)))
    return base * rising


def draw_frame_mass(key, part):
    key = jax.random.fold_in(key, 21)
    return rising_mass(key, NF)


def draw_token_mass(key, part):
    key = jax.random.fold_in(key, 31)
    return rising_mass(key, NT)


def setup_inputs(seed: int = 0) -> dict:
    streams_of = jax.random.split(jax.random.key(seed), 5)
    return {
        "frames": draw_frames(jax.random.fold_in(streams_of[4], 71), 0),
        "tokens": draw_tokens(jax.random.fold_in(streams_of[4], 71), 0),
        "frame_mass": draw_frame_mass(jax.random.fold_in(streams_of[4], 71), 0),
        "token_mass": draw_token_mass(jax.random.fold_in(streams_of[4], 71), 0),
    }


def combine(earlier, later):
    highest = jnp.maximum(earlier[0], later[0])
    return (highest, earlier[1] * jnp.exp(earlier[0] - highest) + later[1] * jnp.exp(later[0] - highest))

def reference(frames, tokens, frame_mass, token_mass):
    score_scale = 1.0 / math.sqrt(D)
    frame_share = frame_mass / jnp.sum(frame_mass)
    log_frame = jnp.log(frame_share)
    log_token = jnp.log(token_mass / jnp.sum(token_mass))
    blocks = frames.reshape(NF // F_DEV, F_DEV, D)
    log_blocks = log_frame.reshape(NF // F_DEV, F_DEV)
    share_blocks = frame_share.reshape(NF // F_DEV, F_DEV)

    def block_scores(block):
        return lax.dot_general(block, tokens, (((1,), (1,)), ((), ())), preferred_element_type=jnp.float32) * score_scale
    token_pot = jnp.zeros((NT,), jnp.float32)
    frame_pot = jnp.zeros((NF // F_DEV, F_DEV), jnp.float32)
    for step_index in range(ITERS):

        def row_pass(pair):
            shifted = block_scores(pair[0]) + token_pot[None, :]
            highest = lax.optimization_barrier(jnp.max(shifted, axis=1))
            summed = lax.optimization_barrier(jnp.sum(jnp.exp(shifted - highest[:, None]), axis=1))
            return pair[1] - (highest + jnp.log(summed))
        frame_pot = lax.map(row_pass, (blocks, log_blocks))

        def col_pass(carry, pair):
            shifted = block_scores(pair[0]) + pair[1][:, None]
            highest = lax.optimization_barrier(jnp.max(shifted, axis=0))
            summed = lax.optimization_barrier(jnp.sum(jnp.exp(shifted - highest[None, :]), axis=0))
            return (combine(carry, (highest, summed)), None)
        start_carry = (jnp.full((NT,), -jnp.inf, jnp.float32), jnp.zeros((NT,), jnp.float32))
        (highest, summed), unused = lax.scan(col_pass, start_carry, (blocks, frame_pot))
        token_pot = log_token - (highest + jnp.log(summed))

    def final_pass(carry, triple):
        block, potential, share = triple
        weights = jnp.exp(block_scores(block) + potential[:, None] + token_pot[None, :])
        row_sum = lax.optimization_barrier(jnp.sum(weights, axis=1))
        transport = weights.astype(jnp.bfloat16)
        frame_whole = jnp.dot(transport, tokens, preferred_element_type=jnp.float32)
        token_part = lax.dot_general(transport, block, (((0,), (0,)), ((), ())), preferred_element_type=jnp.float32)
        new_carry = (carry[0] + token_part, carry[1] + lax.optimization_barrier(jnp.sum(weights, axis=0)))
        return (new_carry, ((frame_whole / row_sum[:, None]).astype(jnp.bfloat16), row_sum / share))
    start_final = (jnp.zeros((NT, D), jnp.float32), jnp.zeros((NT,), jnp.float32))
    (token_whole, col_sum), (frame_map, mass_ratio) = lax.scan(final_pass, start_final, (blocks, frame_pot, share_blocks))
    token_map = (token_whole / col_sum[:, None]).astype(jnp.bfloat16)
    return (frame_map.reshape(NF, D), token_map, mass_ratio.reshape(NF))
```

```python
import functools
import math

import jax
import jax.numpy as jnp
from jax import lax
from jax.experimental import pallas as pl
from jax.experimental.pallas import tpu as pltpu
from jax.sharding import PartitionSpec as P

F32, BF16 = jnp.float32, jnp.bfloat16
TILE = 256
VMEM_BYTES = 48 * 1024 * 1024


def swap(value, axis, bit):
    size = lax.axis_size(axis)
    return lax.ppermute(value, axis, [(i, i ^ bit) for i in range(size)])


def log2(x):
    return jnp.log(x) * (1.0 / math.log(2.0))


def contract_last(a, b):
    return lax.dot_general(a, b, (((1,), (1,)), ((), ())), preferred_element_type=F32)


def column(row, out_ref):
    for start in range(0, row.shape[1], 128):
        block = jnp.broadcast_to(row[:, start : start + 128], (128, 128))
        out_ref[start : start + 128, :] = block.T


def lane_sum_row(p):
    part = p[:, 0:128]
    for start in range(128, p.shape[1], 128):
        part = part + p[:, start : start + 128]
    total = jnp.sum(part.T, axis=0, keepdims=True)
    return total


def merge_lse(parts):
    highest = jnp.max(parts, axis=0, keepdims=True)
    return highest + log2(jnp.sum(jnp.exp2(parts - highest), axis=0, keepdims=True))


def first_rows(scale, t_ref, f_ref, lse_ref, s_ref):
    s_ref[...] = contract_last(t_ref[...], f_ref[...]) * scale
    s = s_ref[...]
    highest = jnp.max(s, axis=0, keepdims=True)
    lse_ref[...] = highest + log2(jnp.sum(jnp.exp2(s - highest), axis=0, keepdims=True))


def first_cols(scale, lse_parts_ref, fm_ref, f_ref, t_ref, lse_ref, u_ref, s_ref, col_ref):
    @pl.when(pl.program_id(0) == 0)
    def _():
        u = log2(fm_ref[...]) - merge_lse(lse_parts_ref[...])
        u_ref[...] = u
        column(u, col_ref)

    s = contract_last(f_ref[...], t_ref[...]) * scale
    bias = col_ref[...]
    s_ref[...] = s + jnp.concatenate([bias] * (s.shape[1] // 128), axis=1)
    s = s_ref[...]
    highest = jnp.max(s, axis=0, keepdims=True)
    lse_ref[...] = highest + log2(jnp.sum(jnp.exp2(s - highest), axis=0, keepdims=True))


def second_rows(scale, lse_parts_ref, tm_ref, u_ref, t_ref, f_ref, sum_ref, v_ref, col_ref):
    @pl.when(pl.program_id(0) == 0)
    def _():
        v = log2(tm_ref[...]) - merge_lse(lse_parts_ref[...])
        v_ref[...] = v
        column(v, col_ref)

    s = contract_last(t_ref[...], f_ref[...]) * scale
    bias = col_ref[...]
    x = s + jnp.concatenate([bias] * (s.shape[1] // 128), axis=1) + u_ref[...]
    sum_ref[...] = jnp.sum(jnp.exp2(x), axis=0, keepdims=True)


def second_cols(scale, row_parts_ref, fm_ref, u_ref, v_ref, t_ref, f_ref, sum_ref, acc_ref, u2_ref, col_ref):
    @pl.when(pl.program_id(0) == 0)
    def _():
        u2_ref[...] = u_ref[...] + log2(fm_ref[...] / jnp.sum(row_parts_ref[...], axis=0, keepdims=True))

    column(v_ref[...], col_ref)
    s = contract_last(t_ref[...], f_ref[...]) * scale
    bias = col_ref[...]
    x = s + jnp.concatenate([bias] * (s.shape[1] // 128), axis=1) + u2_ref[...]
    p = jnp.exp2(x)
    sum_ref[...] = lane_sum_row(p)
    acc_ref[...] = jnp.dot(p.astype(BF16), f_ref[...], preferred_element_type=F32).astype(BF16)


def last_rows(scale, col_parts_ref, tm_ref, v_ref, u2_ref, shift_ref, f_ref, t_ref, sum_ref, acc_ref, total_ref, v2_ref, col_ref):
    @pl.when(pl.program_id(0) == 0)
    def _():
        total = jnp.sum(col_parts_ref[...], axis=0, keepdims=True)
        total_ref[...] = total
        v2_ref[...] = v_ref[...] + log2(tm_ref[...] / total)

    column(u2_ref[...] + shift_ref[0, 0], col_ref)
    s = contract_last(f_ref[...], t_ref[...]) * scale
    bias = col_ref[...]
    x = s + jnp.concatenate([bias] * (s.shape[1] // 128), axis=1) + v2_ref[...]
    p = jnp.exp2(x)
    sum_ref[...] = lane_sum_row(p)
    acc_ref[...] = jnp.dot(p.astype(BF16), t_ref[...], preferred_element_type=F32).astype(BF16)


def whole(shape):
    return pl.BlockSpec(shape, lambda i: (0,) * len(shape))


def lanes():
    return pl.BlockSpec((1, TILE), lambda i: (0, i))


def rows(width):
    return pl.BlockSpec((TILE, width), lambda i: (i, 0))


def row_shape(n):
    return jax.ShapeDtypeStruct((1, n), F32)


def call(body, steps, in_specs, out_specs, out_shape, scratch, name):
    return pl.pallas_call(
        body,
        grid=(steps,),
        in_specs=in_specs,
        out_specs=out_specs,
        out_shape=out_shape,
        scratch_shapes=scratch,
        compiler_params=pltpu.CompilerParams(vmem_limit_bytes=VMEM_BYTES),
        name=name,
    )


def shards(frames, tokens, frame_mass, token_mass):
    nf, d = frames.shape
    nt = tokens.shape[0]
    n_ctx = lax.axis_size("ctx")
    scale = math.log2(math.e) / math.sqrt(d)
    fm, tm = frame_mass.reshape(1, nf), token_mass.reshape(1, nt)
    f_steps, t_steps = nf // TILE, nt // TILE
    f_all, t_all = whole((nf, d)), whole((nt, d))

    lse = call(
        functools.partial(first_rows, scale), f_steps, [t_all, rows(d)], lanes(), row_shape(nf),
        [pltpu.VMEM((nt, TILE), F32)], "first_rows",
    )(tokens, frames)
    with jax.named_scope("rows_one"):
        own_token_mass = jnp.sum(token_mass)
        lse = lax.all_gather(lse, "tok", tiled=True)
    lse, u = call(
        functools.partial(first_cols, scale), t_steps,
        [whole((4, nf)), whole((1, nf)), f_all, rows(d)], [lanes(), whole((1, nf))], [row_shape(nt), row_shape(nf)],
        [pltpu.VMEM((nf, TILE), F32), pltpu.VMEM((nf, 128), F32)], "first_cols",
    )(lse, fm, frames, tokens)
    with jax.named_scope("cols_one"):
        packed = jnp.concatenate([lse, jnp.broadcast_to(jnp.sum(frame_mass), (1, 128))], axis=1)
        packed = jnp.broadcast_to(packed[None], (n_ctx, 1, nt + 128))
        packed = lax.all_to_all(packed, "ctx", 0, 0)[:, 0]
        lse = packed[:, :nt]
        frame_total = jnp.sum(packed[:, nt])
    part, v = call(
        functools.partial(second_rows, scale), f_steps,
        [whole((n_ctx, nt)), whole((1, nt)), lanes(), t_all, rows(d)], [lanes(), whole((1, nt))],
        [row_shape(nf), row_shape(nt)], [pltpu.VMEM((nt, 128), F32)], "second_rows",
    )(lse, tm, u, tokens, frames)
    with jax.named_scope("rows_two"):
        packed = jnp.concatenate([part, jnp.broadcast_to(own_token_mass, (1, 128))], axis=1)
        packed = lax.all_gather(packed, "tok", tiled=True)
        part = packed[:, :nf]
        row_one = jnp.sum(part, axis=0)
        token_total = jnp.sum(packed[:, nf])
    part, token_part, u2 = call(
        functools.partial(second_cols, scale), t_steps,
        [whole((4, nf)), whole((1, nf)), whole((1, nf)), lanes(), rows(d), f_all],
        [lanes(), rows(d), whole((1, nf))],
        [row_shape(nt), jax.ShapeDtypeStruct((nt, d), BF16), row_shape(nf)], [pltpu.VMEM((TILE, 128), F32)], "second_cols",
    )(part, fm, u, v, tokens, frames)
    with jax.named_scope("cols_two"):
        part = lax.all_to_all(jnp.broadcast_to(part[None], (n_ctx, 1, nt)), "ctx", 0, 0)[:, 0]
    shift = -log2(token_total).reshape(1, 1)
    part, frame_part, col_total, v2 = call(
        functools.partial(last_rows, scale), f_steps,
        [whole((n_ctx, nt)), whole((1, nt)), whole((1, nt)), lanes(),
         pl.BlockSpec(memory_space=pltpu.SMEM), rows(d), t_all],
        [lanes(), rows(d), whole((1, nt)), whole((1, nt))],
        [row_shape(nf), jax.ShapeDtypeStruct((nf, d), BF16), row_shape(nt), row_shape(nt)],
        [pltpu.VMEM((TILE, 128), F32)], "last_rows",
    )(part, tm, v, u2, shift, frames, tokens)

    with jax.named_scope("frame_sums"):
        row_sum = jnp.sum(lax.all_gather(part, "tok", tiled=True), axis=0)
        core = lax.axis_index("tok") % 2
        half = nf // 2
        mine = lax.dynamic_slice_in_dim(frame_part, core * half, half)
        theirs = lax.dynamic_slice_in_dim(frame_part, (1 - core) * half, half)
        mine = (mine.astype(F32) + swap(theirs, "tok", 1).astype(F32)).astype(BF16)
        other = swap(mine, "tok", 2)
    with jax.named_scope("token_sums"):
        pieces = lax.all_to_all(token_part.reshape(n_ctx, nt // n_ctx, d), "ctx", 0, 0)
        me = lax.axis_index("ctx")
        own = nt // n_ctx
        total = jnp.sum(pieces.astype(F32), axis=0)
        total = total / lax.dynamic_slice_in_dim(col_total[0], me * own, own)[:, None]
        piece = total.astype(BF16)
        token_map = lax.all_to_all(jnp.broadcast_to(piece[None], (n_ctx, own, d)), "ctx", 0, 0).reshape(nt, d)
    with jax.named_scope("frame_out"):
        done = mine.astype(F32) + other.astype(F32)
        done = (done / lax.dynamic_slice_in_dim(row_sum, core * half, half)[:, None]).astype(BF16)
        sibling = swap(done, "tok", 1)
        low = jnp.where(core == 0, done, sibling)
        high = jnp.where(core == 0, sibling, done)
        frame_map = jnp.concatenate([low, high])
    mass_ratio = row_sum / (frame_mass / frame_total)
    return frame_map, token_map, mass_ratio


def solution(mesh):
    return jax.shard_map(
        shards,
        mesh=mesh,
        in_specs=(P("ctx", None), P("tok", None), P("ctx"), P("tok")),
        out_specs=(P("ctx", None), P("tok", None), P("ctx")),
        check_vma=False,
    )
```

```python
import functools
import math

import jax
import jax.numpy as jnp
from jax import lax
from jax.experimental import pallas as pl
from jax.experimental.pallas import tpu as pltpu
from jax.sharding import PartitionSpec as P

F32, BF16 = jnp.float32, jnp.bfloat16
W = 512
TOK = 256
CHUNK = 128
EXTRA = 256
VMEM_BYTES = 20 * 1024 * 1024
X, Y, Z = 1, 4, 16
VMEM = pl.BlockSpec(memory_space=pltpu.VMEM)
SMEM = pl.BlockSpec(memory_space=pltpu.SMEM)
ANY = pl.BlockSpec(memory_space=pl.ANY)


def swap_tok(value, bit):
    return lax.ppermute(value, "tok", [(i, i ^ bit) for i in range(lax.axis_size("tok"))])


def shift(value, stride, step, size=4):
    pairs = []
    for i in range(lax.axis_size("ctx")):
        c = i // stride % size
        pairs.append((i, i + ((c + step) % size - c) * stride))
    return lax.ppermute(value, "ctx", pairs)


def log2(x):
    return jnp.log(x) * (1.0 / math.log(2.0))


def column(row, out_ref):
    for start in range(0, row.shape[1], 128):
        block = jnp.broadcast_to(row[:, start : start + 128], (128, 128))
        out_ref[start : start + 128, :] = block.T


def wide(col, width):
    return jnp.concatenate([col] * (width // 128), axis=1)


def merge_lse(parts):
    highest = jnp.max(parts, axis=0, keepdims=True)
    return highest + log2(jnp.sum(jnp.exp2(parts - highest), axis=0, keepdims=True))


def row_slice(i, size):
    return pl.ds(pl.multiple_of(i * size, size), size)


def first_rows(scale, t_ref, f_ref, lse_ref, s_ref):
    i = pl.program_id(0)
    s_ref[i] = (
        lax.dot_general(t_ref[...], f_ref[...], (((1,), (1,)), ((), ())), preferred_element_type=F32) * scale
    )
    highest = total = None
    for c in range(0, t_ref.shape[0], CHUNK):
        s = s_ref[i, c : c + CHUNK, :].reshape(CHUNK // 8, 8, W)
        top = jnp.max(s, axis=0)
        if highest is None:
            highest = top
            total = jnp.sum(jnp.exp2(s - highest[None]), axis=0)
        else:
            top = jnp.maximum(highest, top)
            total = total * jnp.exp2(highest - top) + jnp.sum(jnp.exp2(s - top[None]), axis=0)
            highest = top
    top = jnp.max(highest, axis=0, keepdims=True)
    lse_ref[...] = top + log2(jnp.sum(total * jnp.exp2(highest - top), axis=0, keepdims=True))


def first_cols(s_ref, parts_ref, fm_ref, lse_ref, u_ref):
    i = pl.program_id(0)
    nt = s_ref.shape[1]

    @pl.when(i == 0)
    def _():
        u_ref[...] = log2(fm_ref[...]) - merge_lse(parts_ref[...])
        lse_ref[:, :, nt:] = jnp.broadcast_to(jnp.sum(fm_ref[...]).reshape(1, 1, 1), (lse_ref.shape[0], 1, EXTRA))

    step = 64
    found = []
    for r in range(0, TOK, step):
        rows = pl.ds(pl.multiple_of(i * TOK + r, step), step)
        highest = total = None
        for c in range(s_ref.shape[0]):
            for w in range(0, W, 256):
                lane = c * W + w
                s = s_ref[c, rows, w : w + 256] + u_ref[:, lane : lane + 256]
                low, high = s[:, :128], s[:, 128:]
                top = jnp.maximum(low, high)
                if highest is None:
                    highest = top
                    total = jnp.exp2(low - highest) + jnp.exp2(high - highest)
                else:
                    top = jnp.maximum(highest, top)
                    total = total * jnp.exp2(highest - top) + (jnp.exp2(low - top) + jnp.exp2(high - top))
                    highest = top
        top = jnp.max(highest, axis=1, keepdims=True)
        lse = top + log2(jnp.sum(total * jnp.exp2(highest - top), axis=1, keepdims=True))
        found.append(jnp.broadcast_to(lse, (step, 128)))
    row = jnp.concatenate(found).T[0:1]
    lse_ref[:, :, row_slice(i, TOK)] = jnp.broadcast_to(row[None], (lse_ref.shape[0], 1, TOK))


def second_rows(s_ref, parts_ref, tm_ref, u_ref, sum_ref, v_ref, mass_ref, e_ref, col_ref):
    i = pl.program_id(0)
    nt = s_ref.shape[1]
    nf = u_ref.shape[1]

    @pl.when(i == 0)
    def _():
        v = log2(tm_ref[...]) - merge_lse(parts_ref[:, :nt])
        v_ref[...] = v
        column(v, col_ref)
        mass_ref[...] = jnp.sum(parts_ref[:, nt : nt + 128], axis=0, keepdims=True)
        sum_ref[:, nf:] = jnp.broadcast_to(jnp.sum(tm_ref[...]).reshape(1, 1), (1, EXTRA))

    u = u_ref[:, row_slice(i, W)]
    total = None
    for c in range(0, nt, CHUNK):
        e = jnp.exp2(s_ref[i, c : c + CHUNK, :] + wide(col_ref[c : c + CHUNK, :], W) + u)
        e_ref[i, c : c + CHUNK, :] = e
        part = jnp.sum(e.reshape(CHUNK // 8, 8, W), axis=0)
        total = part if total is None else total + part
    sum_ref[:, row_slice(i, W)] = jnp.sum(total, axis=0, keepdims=True)


def col_sums(e_ref, parts_ref, fm_ref, sum_ref, alpha_ref, share_ref):
    i = pl.program_id(0)
    nf = fm_ref.shape[1]

    @pl.when(i == 0)
    def _():
        total = jnp.sum(parts_ref[...], axis=0, keepdims=True)
        alpha = fm_ref[...] / total[:, :nf]
        alpha_ref[...] = alpha
        share_ref[...] = alpha / wide(total[:, nf : nf + 128], nf)

    step = 64
    found = []
    for r in range(0, TOK, step):
        rows = pl.ds(pl.multiple_of(i * TOK + r, step), step)
        total = None
        for c in range(e_ref.shape[0]):
            p = e_ref[c, rows, :] * alpha_ref[:, c * W : (c + 1) * W]
            for w in range(0, W, 128):
                part = p[:, w : w + 128]
                total = part if total is None else total + part
        found.append(total)
    row = jnp.sum(jnp.concatenate(found).T, axis=0, keepdims=True)
    sum_ref[:, :, row_slice(i, TOK)] = jnp.broadcast_to(row[None], (sum_ref.shape[0], 1, TOK))


def token_parts(e_ref, alpha_ref, f_ref, out_ref):
    rows = row_slice(pl.program_id(0), TOK)
    acc = None
    for c in range(e_ref.shape[0]):
        p = (e_ref[c, rows, :] * alpha_ref[:, c * W : (c + 1) * W]).astype(BF16)
        part = jnp.dot(p, f_ref[c * W : (c + 1) * W, :], preferred_element_type=F32)
        acc = part if acc is None else acc + part
    out_ref[...] = acc.astype(BF16)


def frame_parts(base_ref, e_ref, parts_ref, tm_ref, share_ref, tt_ref, sum_ref, out_ref, total_ref, col_ref):
    i = pl.program_id(0)

    @pl.when(i == 0)
    def _():
        total = jnp.sum(parts_ref[...], axis=0, keepdims=True)
        total_ref[...] = total
        column(tm_ref[...] / total, col_ref)

    slab = base_ref[0] + i
    share = share_ref[:, row_slice(slab, W)]
    p = e_ref[slab] * wide(col_ref[...], W) * share
    sum_ref[...] = jnp.sum(p, axis=0, keepdims=True)
    out_ref[...] = jnp.dot(tt_ref[...], p.astype(BF16), preferred_element_type=F32).T.astype(BF16)


def place_tokens(place_ref, *refs):
    parts, out_ref, sems = refs[:8], refs[8], refs[9]
    x, y = place_ref[0], place_ref[1]
    block = parts[0].shape[0]
    piece = block // 4
    copies = []
    for side, (outer, inner) in enumerate(((x, y), (y, x))):
        for k in range(4):
            for j in range(4):
                start = side * 4 * block + lax.rem(outer + k, 4) * block + lax.rem(inner + j, 4) * piece
                copies.append(
                    pltpu.make_async_copy(
                        parts[side * 4 + k].at[pl.ds(j * piece, piece), :],
                        out_ref.at[pl.ds(pl.multiple_of(start, piece), piece), :],
                        sems.at[len(copies)],
                    )
                )
    for copy in copies:
        copy.start()
    for copy in copies:
        copy.wait()


def place_frames(core_ref, mine_ref, theirs_ref, out_ref, sems):
    half = mine_ref.shape[0]
    copies = []
    for k, ref in enumerate((mine_ref, theirs_ref)):
        start = lax.rem(core_ref[0] + k, 2) * half
        copies.append(
            pltpu.make_async_copy(ref, out_ref.at[pl.ds(pl.multiple_of(start, half), half), :], sems.at[k])
        )
    for copy in copies:
        copy.start()
    for copy in copies:
        copy.wait()


def whole(*shape):
    return pl.BlockSpec(shape, lambda i: (0,) * len(shape))


def rows(size, width):
    return pl.BlockSpec((size, width), lambda i: (i, 0))


def lanes(size):
    return pl.BlockSpec((1, size), lambda i: (0, i))


def f32(*shape):
    return jax.ShapeDtypeStruct(shape, F32)


def call(body, steps, in_specs, out_specs, out_shape, scratch=(), **kwargs):
    return pl.pallas_call(
        body,
        grid=(steps,),
        in_specs=in_specs,
        out_specs=out_specs,
        out_shape=out_shape,
        scratch_shapes=scratch,
        compiler_params=pltpu.CompilerParams(vmem_limit_bytes=VMEM_BYTES),
        **kwargs,
    )


def at(blocks, index):
    return lax.dynamic_index_in_dim(blocks, lax.rem(index, 4), keepdims=False)


def scatter(blocks, me, stride):
    total = at(blocks, me).astype(F32)
    for step in (1, 3, 2):
        total = total + shift(at(blocks, me + step), stride, step).astype(F32)
    return total.astype(BF16)


def gather(block, stride):
    return [block] + [shift(block, stride, -k) for k in (1, 2, 3)]


def shards(frames, tokens, frame_mass, token_mass):
    nf, d = frames.shape
    nt = tokens.shape[0]
    n_ctx, n_tok = lax.axis_size("ctx"), lax.axis_size("tok")
    scale = math.log2(math.e) / math.sqrt(d)
    fm, tm = frame_mass.reshape(1, nf), token_mass.reshape(1, nt)
    slabs, steps = nf // W, nt // TOK
    kept = pltpu.VMEM((slabs, nt, W), F32)
    ctx, core = lax.axis_index("ctx"), lax.axis_index("tok") % 2
    x, y = ctx % 4, ctx // 4 % 4

    lse, s = call(
        functools.partial(first_rows, scale), slabs, [whole(nt, d), rows(W, d)], [lanes(W), VMEM], [f32(1, nf), kept],
        name="first_rows",
    )(tokens, frames)
    with jax.named_scope("rows_one"):
        lse = lax.all_gather(lse, "tok", tiled=True)
    lse, u = call(
        first_cols, steps, [VMEM, whole(n_tok, nf), whole(1, nf)], [whole(n_ctx, 1, nt + EXTRA), whole(1, nf)],
        [f32(n_ctx, 1, nt + EXTRA), f32(1, nf)], name="first_cols",
    )(s, lse, fm)
    tokens_later, lse = lax.optimization_barrier((tokens, lse))
    with jax.named_scope("cols_one"):
        lse = lax.all_to_all(lse, "ctx", 0, 0)[:, 0]
    turned = tokens_later.T
    part, v, frame_total, e = call(
        second_rows, slabs, [VMEM, whole(n_ctx, nt + EXTRA), whole(1, nt), whole(1, nf)],
        [whole(1, nf + EXTRA), whole(1, nt), whole(1, 128), VMEM],
        [f32(1, nf + EXTRA), f32(1, nt), f32(1, 128), kept], [pltpu.VMEM((nt, 128), F32)],
        input_output_aliases={0: 3}, name="second_rows",
    )(s, lse, tm, u)
    with jax.named_scope("rows_two"):
        part = lax.all_gather(part, "tok", tiled=True)
    part, alpha, share = call(
        col_sums, steps, [VMEM, whole(n_tok, nf + EXTRA), whole(1, nf)],
        [whole(n_ctx, 1, nt), whole(1, nf), whole(1, nf)], [f32(n_ctx, 1, nt), f32(1, nf), f32(1, nf)], name="col_sums",
    )(e, part, fm)
    with jax.named_scope("cols_two"):
        part = lax.all_to_all(part, "ctx", 0, 0)[:, 0]
    token_part = call(
        token_parts, steps, [VMEM, whole(1, nf), whole(nf, d)], rows(TOK, d), jax.ShapeDtypeStruct((nt, d), BF16),
        name="token_parts",
    )(e, alpha, frames)

    def frame_half(which):
        base = (which * (slabs // 2)).reshape(1).astype(jnp.int32)
        return call(
            frame_parts, slabs // 2, [SMEM, VMEM, whole(n_ctx, nt), whole(1, nt), whole(1, nf), whole(d, nt)],
            [lanes(W), rows(W, d), whole(1, nt)],
            [f32(1, nf // 2), jax.ShapeDtypeStruct((nf // 2, d), BF16), f32(1, nt)], [pltpu.VMEM((nt, 128), F32)],
            name="frame_parts",
        )(base, e, part, tm, share, turned)

    with jax.named_scope("token_scatter"):
        half = token_part.reshape(2, 4, nt // 8, d)
        a = scatter(half[0], x, X)
        b = scatter(half[1], y, Y)
        a = scatter(a.reshape(4, nt // 32, d), y, Y)
        b = scatter(b.reshape(4, nt // 32, d), x, X)
        both = jnp.stack([a, b])
        both = both.astype(F32) + shift(both, Z, 1, 2).astype(F32)
    with jax.named_scope("frames_first_half"):
        their_sum, theirs, _ = frame_half(1 - core)
        theirs = swap_tok(theirs, 1)
    my_sum, mine, col_total = frame_half(core)
    with jax.named_scope("frame_rows"):
        my_sum = my_sum + swap_tok(their_sum, 1)
        mine = (mine.astype(F32) + theirs.astype(F32)).astype(BF16)
        my_sum = my_sum + swap_tok(my_sum, 2)
        other = swap_tok(mine, 2)
    with jax.named_scope("token_gather"):
        piece = nt // 32
        sums = [
            lax.dynamic_slice_in_dim(col_total[0], start, piece)
            for start in (x * 4 * piece + y * piece, nt // 2 + y * 4 * piece + x * piece)
        ]
        both = (both / jnp.stack(sums)[:, :, None]).astype(BF16)
        a = gather(jnp.concatenate(gather(both[0], Y)), X)
        b = gather(jnp.concatenate(gather(both[1], X)), Y)
        place = jnp.stack([x, y]).astype(jnp.int32)
        token_map = pl.pallas_call(
            place_tokens, in_specs=[SMEM] + [ANY] * 8, out_specs=ANY, out_shape=jax.ShapeDtypeStruct((nt, d), BF16),
            scratch_shapes=[pltpu.SemaphoreType.DMA((32,))], name="place_tokens",
        )(place, *a, *b)
    with jax.named_scope("frame_out"):
        mine = ((mine.astype(F32) + other.astype(F32)) / my_sum.reshape(-1, 1)).astype(BF16)
        theirs = swap_tok(mine, 1)
        their_sum = swap_tok(my_sum, 1)
        frame_map = pl.pallas_call(
            place_frames, in_specs=[SMEM, ANY, ANY], out_specs=ANY, out_shape=jax.ShapeDtypeStruct((nf, d), BF16),
            scratch_shapes=[pltpu.SemaphoreType.DMA((2,))], name="place_frames",
        )(core.reshape(1).astype(jnp.int32), mine, theirs)
        low = jnp.where(core == 0, my_sum, their_sum)
        high = jnp.where(core == 0, their_sum, my_sum)
        row_sum = jnp.concatenate([low, high], axis=1)[0]
        mass_ratio = row_sum / (frame_mass / frame_total[0, 0])
    return frame_map, token_map, mass_ratio


def solution(mesh):
    return jax.shard_map(
        shards,
        mesh=mesh,
        in_specs=(P("ctx", None), P("tok", None), P("ctx"), P("tok")),
        out_specs=(P("ctx", None), P("tok", None), P("ctx")),
        check_vma=False,
    )
```

```python
import functools
import math

import jax
import jax.numpy as jnp
from jax import lax
from jax.experimental import pallas as pl
from jax.experimental.pallas import tpu as pltpu
from jax.sharding import PartitionSpec as P

F32, BF16 = jnp.float32, jnp.bfloat16
W = 256
TOK = 256
CHUNK = 128
SPLIT = 4
HELD = 4
EXTRA = 256
ORDER = ((16, 2), (1, 4), (4, 4))
VMEM_BYTES = 20 * 1024 * 1024
VMEM = pl.BlockSpec(memory_space=pltpu.VMEM)
SMEM = pl.BlockSpec(memory_space=pltpu.SMEM)
ANY = pl.BlockSpec(memory_space=pl.ANY)


def swap_tok(value, bit):
    return lax.ppermute(value, "tok", [(i, i ^ bit) for i in range(lax.axis_size("tok"))])


def shift(value, stride, step, size):
    pairs = []
    for i in range(lax.axis_size("ctx")):
        c = i // stride % size
        pairs.append((i, i + ((c + step) % size - c) * stride))
    return lax.ppermute(value, "ctx", pairs)


def log2(x):
    return jnp.log(x) * (1.0 / math.log(2.0))


def column(row, out_ref):
    for start in range(0, row.shape[1], 128):
        block = jnp.broadcast_to(row[:, start : start + 128], (128, 128))
        out_ref[start : start + 128, :] = block.T


def wide(col, width):
    return jnp.concatenate([col] * (width // 128), axis=1)


def merge_lse(parts):
    highest = functools.reduce(jnp.maximum, parts)
    return highest + log2(sum(jnp.exp2(part - highest) for part in parts))


def ring(value, stride, size):
    return [value] + [shift(value, stride, step, size) for step in range(1, size)]


def row_slice(i, size):
    return pl.ds(pl.multiple_of(i * size, size), size)


def turn(in_ref, out_ref):
    out_ref[...] = in_ref[...].T


def first_rows(scale, *refs):
    t_refs, (f_ref, lse_ref, s_ref) = refs[:SPLIT], refs[SPLIT:]
    i = pl.program_id(0)
    tokens = jnp.concatenate([t_ref[...] for t_ref in t_refs])
    s_ref[i] = (
        lax.dot_general(tokens, f_ref[...], (((1,), (1,)), ((), ())), preferred_element_type=F32) * scale
    )
    highest = total = None
    for c in range(0, tokens.shape[0], CHUNK):
        s = s_ref[i, c : c + CHUNK, :].reshape(CHUNK // 8, 8, W)
        top = jnp.max(s, axis=0)
        if highest is None:
            highest = top
            total = jnp.sum(jnp.exp2(s - highest[None]), axis=0)
        else:
            top = jnp.maximum(highest, top)
            total = total * jnp.exp2(highest - top) + jnp.sum(jnp.exp2(s - top[None]), axis=0)
            highest = top
    top = jnp.max(highest, axis=0, keepdims=True)
    lse_ref[...] = top + log2(jnp.sum(total * jnp.exp2(highest - top), axis=0, keepdims=True))


def first_cols(s_ref, all_ref, fm_ref, lse_ref, u_ref, mass_ref):
    i = pl.program_id(0)

    @pl.when(i == 0)
    def _():
        u_ref[...] = log2(fm_ref[...]) - all_ref[...]
        mass_ref[...] = jnp.broadcast_to(jnp.sum(fm_ref[...]).reshape(1, 1), (1, 128))

    step = 16
    found = []
    for r in range(0, TOK, step):
        rows = pl.ds(pl.multiple_of(i * TOK + r, step), step)
        tiles = [
            s_ref[c, rows, w : w + 128] + u_ref[:, c * W + w : c * W + w + 128]
            for c in range(s_ref.shape[0])
            for w in range(0, W, 128)
        ]
        highest = functools.reduce(jnp.maximum, tiles)
        total = sum(jnp.exp2(tile - highest) for tile in tiles)
        top = jnp.max(highest, axis=1, keepdims=True)
        lse = top + log2(jnp.sum(total * jnp.exp2(highest - top), axis=1, keepdims=True))
        found.append(jnp.broadcast_to(lse, (step, 128)))
    lse_ref[...] = jnp.concatenate(found).T[0:1]


def second_rows(s_ref, all_ref, tm_ref, u_ref, sum_ref, e_ref, col_ref):
    i = pl.program_id(0)
    nt = s_ref.shape[1]
    nf = u_ref.shape[1]

    @pl.when(i == 0)
    def _():
        column(log2(tm_ref[...]) - all_ref[...], col_ref)
        sum_ref[:, nf:] = jnp.broadcast_to(jnp.sum(tm_ref[...]).reshape(1, 1), (1, EXTRA))

    u = u_ref[:, row_slice(i, W)]
    total = None
    for c in range(0, nt, CHUNK):
        e = jnp.exp2(s_ref[i, c : c + CHUNK, :] + wide(col_ref[c : c + CHUNK, :], W) + u)
        e_ref[i, c : c + CHUNK, :] = e
        part = jnp.sum(e.reshape(CHUNK // 8, 8, W), axis=0)
        total = part if total is None else total + part
    sum_ref[:, row_slice(i, W)] = jnp.sum(total, axis=0, keepdims=True)


def second_cols(e_ref, total_ref, fm_ref, f_ref, sum_ref, out_ref, share_ref, stored_ref, alpha_ref, sems):
    i = pl.program_id(0)
    nf = fm_ref.shape[1]

    def store(step):
        some = row_slice(step, TOK)
        return pltpu.make_async_copy(e_ref.at[:, some, :], stored_ref.at[:, some, :], sems.at[step])

    store(i).start()

    @pl.when(i == 0)
    def _():
        alpha = fm_ref[...] / total_ref[:, :nf]
        alpha_ref[...] = alpha
        share_ref[...] = alpha / wide(total_ref[:, nf : nf + 128], nf)

    rows = row_slice(i, TOK)
    acc = total = None
    for c in range(e_ref.shape[0]):
        p = e_ref[c, rows, :] * alpha_ref[:, c * W : (c + 1) * W]
        part = p[:, :128]
        for w in range(128, W, 128):
            part = part + p[:, w : w + 128]
        total = part if total is None else total + part
        part = jnp.dot(p.astype(BF16), f_ref[c * W : (c + 1) * W, :], preferred_element_type=F32)
        acc = part if acc is None else acc + part
    sum_ref[...] = jnp.sum(total.T, axis=0, keepdims=True)
    out_ref[...] = acc.astype(BF16)

    @pl.when(i == pl.num_programs(0) - 1)
    def _():
        for step in range(e_ref.shape[1] // TOK):
            store(step).wait()


def frame_parts(
    base_ref, e_ref, total_ref, tm_ref, share_ref, tt_ref, sum_ref, out_ref, col_ref, held_ref, sems
):
    i = pl.program_id(0)
    slabs = pl.num_programs(0)

    def fetch(k):
        slot = lax.rem(k, HELD)
        return pltpu.make_async_copy(e_ref.at[lax.rem(base_ref[0] + k, slabs)], held_ref.at[slot], sems.at[slot])

    @pl.when(i == 0)
    def _():
        for k in range(HELD - 1):
            fetch(k).start()
        column(tm_ref[...] / total_ref[...], col_ref)

    @pl.when(i + HELD - 1 < slabs)
    def _():
        fetch(i + HELD - 1).start()

    fetch(i).wait()
    share = share_ref[:, row_slice(lax.rem(base_ref[0] + i, slabs), W)]
    p = held_ref[lax.rem(i, HELD)] * wide(col_ref[...], W) * share
    sum_ref[...] = jnp.sum(p, axis=0, keepdims=True)
    out_ref[...] = jnp.dot(tt_ref[...], p.astype(BF16), preferred_element_type=F32).T.astype(BF16)


def sum_pieces(*refs):
    out_ref = refs[-1]
    rows = refs[0].shape[1]
    for k, pieces_ref in enumerate(refs[:-1]):
        acc = pieces_ref[0].astype(F32)
        for n in range(1, pieces_ref.shape[0]):
            acc = acc + pieces_ref[n].astype(F32)
        out_ref[k * rows : (k + 1) * rows, :] = acc.astype(BF16)


def finish_pieces(mine_ref, other_ref, total_ref, out_ref, col_ref, done_ref, sems):
    column(total_ref[...], col_ref)
    d = mine_ref.shape[1]
    done = (mine_ref[...].astype(F32) + other_ref[...].astype(F32)) / wide(col_ref[...], d)
    done_ref[...] = done.astype(BF16)
    copies = [pltpu.make_async_copy(done_ref, out_ref.at[k], sems.at[k]) for k in range(out_ref.shape[0])]
    for copy in copies:
        copy.start()
    for copy in copies:
        copy.wait()


def place_tokens(pieces_ref, out_ref, held_ref, sems, out_sems):
    count, rows = pieces_ref.shape[0], pieces_ref.shape[1]
    ins = [pltpu.make_async_copy(pieces_ref.at[k], held_ref.at[k], sems.at[k]) for k in range(count)]
    outs = [
        pltpu.make_async_copy(held_ref.at[k], out_ref.at[k * rows : (k + 1) * rows, :], out_sems.at[k])
        for k in range(count)
    ]
    for copy in ins:
        copy.start()
    for k in range(count):
        ins[k].wait()
        outs[k].start()
    for copy in outs:
        copy.wait()


def finish_frames(mine_ref, other_ref, total_ref, out_ref, col_ref):
    column(total_ref[...], col_ref)
    rows, d = mine_ref.shape
    for r in range(0, rows, 128):
        some = slice(r, r + 128)
        done = (mine_ref[some, :].astype(F32) + other_ref[some, :].astype(F32)) / wide(col_ref[some, :], d)
        out_ref[some, :] = done.astype(BF16)


def place_frames(core_ref, mine_ref, theirs_ref, out_ref, sems):
    half = mine_ref.shape[0]
    copies = []
    for k, ref in enumerate((mine_ref, theirs_ref)):
        start = lax.rem(core_ref[0] + k, 2) * half
        copies.append(
            pltpu.make_async_copy(ref, out_ref.at[pl.ds(pl.multiple_of(start, half), half), :], sems.at[k])
        )
    for copy in copies:
        copy.start()
    for copy in copies:
        copy.wait()


def whole(*shape):
    return pl.BlockSpec(shape, lambda i: (0,) * len(shape))


def rows(size, width):
    return pl.BlockSpec((size, width), lambda i: (i, 0))


def lanes(size):
    return pl.BlockSpec((1, size), lambda i: (0, i))


def f32(*shape):
    return jax.ShapeDtypeStruct(shape, F32)


def call(body, steps, in_specs, out_specs, out_shape, scratch=(), **kwargs):
    return pl.pallas_call(
        body,
        grid=(steps,),
        in_specs=in_specs,
        out_specs=out_specs,
        out_shape=out_shape,
        scratch_shapes=scratch,
        compiler_params=pltpu.CompilerParams(vmem_limit_bytes=VMEM_BYTES),
        **kwargs,
    )


def shards(frames, tokens, frame_mass, token_mass):
    nf, d = frames.shape
    nt = tokens.shape[0]
    n_ctx = lax.axis_size("ctx")
    scale = math.log2(math.e) / math.sqrt(d)
    fm, tm = frame_mass.reshape(1, nf), token_mass.reshape(1, nt)
    slabs, steps = nf // W, nt // TOK
    kept = pltpu.VMEM((slabs, nt, W), F32)
    ctx, core = lax.axis_index("ctx"), lax.axis_index("tok") % 2
    hbm = pl.BlockSpec(memory_space=pltpu.HBM)

    lse, s = call(
        functools.partial(first_rows, scale), slabs,
        [pl.BlockSpec((nt // SPLIT, d), lambda i, k=k: (k, 0)) for k in range(SPLIT)] + [rows(W, d)],
        [lanes(W), VMEM], [f32(1, nf), kept], name="first_rows",
    )(*[pltpu.with_memory_space_constraint(tokens, pltpu.HBM)] * SPLIT, pltpu.with_memory_space_constraint(frames, pltpu.HBM))
    with jax.named_scope("rows_one"):
        lse = merge_lse([lse, swap_tok(lse, 1)])
        lse = merge_lse([lse, swap_tok(lse, 2)])
    lse, u, frame_total = call(
        first_cols, steps, [VMEM, whole(1, nf), whole(1, nf)], [lanes(TOK), whole(1, nf), whole(1, 128)],
        [f32(1, nt), f32(1, nf), f32(1, 128)], name="first_cols",
    )(s, lse, fm)
    tokens_later, lse = lax.optimization_barrier((tokens, lse))
    turned = call(
        turn, 4, [rows(nt // 4, d)], pl.BlockSpec((d, nt // 4), lambda i: (0, i)), jax.ShapeDtypeStruct((d, nt), BF16),
        name="turn",
    )(tokens_later)
    with jax.named_scope("cols_one"):
        lse = jnp.concatenate([lse, frame_total], axis=1)
        for stride, size in ORDER:
            parts = ring(lse, stride, size)
            merged = merge_lse([part[:, :nt] for part in parts])
            lse = jnp.concatenate([merged, sum(part[:, nt:] for part in parts)], axis=1)
        lse, frame_total = lse[:, :nt], lse[0, nt]
        turned, lse = lax.optimization_barrier((turned, lse))
    part, e = call(
        second_rows, slabs, [VMEM, whole(1, nt), whole(1, nt), whole(1, nf)], [whole(1, nf + EXTRA), VMEM],
        [f32(1, nf + EXTRA), kept], [pltpu.VMEM((nt, 128), F32)], input_output_aliases={0: 1}, name="second_rows",
    )(s, lse, tm, u)
    with jax.named_scope("rows_two"):
        part = part + swap_tok(part, 1)
        part = part + swap_tok(part, 2)
    part, token_part, share, e = call(
        second_cols, steps, [VMEM, whole(1, nf + EXTRA), whole(1, nf), whole(nf, d)],
        [lanes(TOK), rows(TOK, d), whole(1, nf), hbm],
        [f32(1, nt), jax.ShapeDtypeStruct((nt, d), BF16), f32(1, nf), pltpu.HBM((slabs, nt, W), F32)],
        [pltpu.VMEM((1, nf), F32), pltpu.SemaphoreType.DMA((steps,))], name="second_cols",
    )(e, part, fm, frames)
    with jax.named_scope("cols_two"):
        col_total = part
        for stride, size in ORDER:
            col_total = sum(ring(col_total, stride, size))
    with jax.named_scope("token_scatter"):
        token_part, col_total = lax.optimization_barrier((token_part, col_total))
        plane, own = 16, nt // 16
        planes = [list(range(z, z + plane)) for z in range(0, n_ctx, plane)]
        pieces = lax.all_to_all(token_part.reshape(plane, own, d), "ctx", 0, 0, axis_index_groups=planes)
        deal = own // (2 * SPLIT)
        piece = call(
            sum_pieces, 2,
            [pl.BlockSpec((plane, deal, d), lambda i, k=k: (0, i * SPLIT + k, 0)) for k in range(SPLIT)],
            rows(own // 2, d), jax.ShapeDtypeStruct((own, d), BF16), name="sum_pieces",
        )(*[pieces] * SPLIT)
        other_piece = shift(piece, 16, 1, 2)

    e = pltpu.with_memory_space_constraint(e, pltpu.HBM)
    half = slabs // 2
    base = ((1 - core) * half).reshape(1).astype(jnp.int32)
    with jax.named_scope("frame_rows"):
        sums, parts = pl.pallas_call(
            frame_parts,
            grid=(slabs,),
            in_specs=[SMEM, hbm, whole(1, nt), whole(1, nt), whole(1, nf), whole(d, nt)],
            out_specs=[lanes(W), rows(W, d)],
            out_shape=[f32(1, nf), jax.ShapeDtypeStruct((nf, d), BF16)],
            scratch_shapes=[
                pltpu.VMEM((nt, 128), F32),
                pltpu.VMEM((HELD, nt, W), F32),
                pltpu.SemaphoreType.DMA((HELD,)),
            ],
            compiler_params=pltpu.CompilerParams(vmem_limit_bytes=VMEM_BYTES),
            name="frame_parts",
        )(base, e, col_total, tm, share, turned)
        my_sum = sums[:, nf // 2 :] + swap_tok(sums[:, : nf // 2], 1)
        mine = (parts[nf // 2 :].astype(F32) + swap_tok(parts[: nf // 2], 1).astype(F32)).astype(BF16)
        mine, my_sum = lax.optimization_barrier((mine, my_sum))
        other_sum = swap_tok(my_sum, 2)
        mine, other_piece, other_sum = lax.optimization_barrier((mine, other_piece, other_sum))
        other = swap_tok(mine, 2)
        my_sum = my_sum + other_sum
    with jax.named_scope("token_gather"):
        col_mine = lax.dynamic_slice_in_dim(col_total, ctx % plane * own, own, axis=1)
        pieces = pl.pallas_call(
            finish_pieces, in_specs=[VMEM] * 3, out_specs=hbm, out_shape=pltpu.HBM((plane, own, d), BF16),
            scratch_shapes=[
                pltpu.VMEM((own, 128), F32),
                pltpu.VMEM((own, d), BF16),
                pltpu.SemaphoreType.DMA((plane,)),
            ],
            compiler_params=pltpu.CompilerParams(vmem_limit_bytes=VMEM_BYTES), name="finish_pieces",
        )(piece, other_piece, col_mine)
        pieces = lax.all_to_all(pieces, "ctx", 0, 0, axis_index_groups=planes)
        token_map = pl.pallas_call(
            place_tokens, in_specs=[hbm], out_specs=hbm, out_shape=pltpu.HBM((nt, d), BF16),
            scratch_shapes=[
                pltpu.VMEM((plane, own, d), BF16),
                pltpu.SemaphoreType.DMA((plane,)),
                pltpu.SemaphoreType.DMA((plane,)),
            ],
            compiler_params=pltpu.CompilerParams(vmem_limit_bytes=VMEM_BYTES), name="place_tokens",
        )(pltpu.with_memory_space_constraint(pieces, pltpu.HBM))
    with jax.named_scope("frame_out"):
        mine = pl.pallas_call(
            finish_frames, in_specs=[VMEM] * 3, out_specs=VMEM, out_shape=jax.ShapeDtypeStruct((nf // 2, d), BF16),
            scratch_shapes=[pltpu.VMEM((nf // 2, 128), F32)],
            compiler_params=pltpu.CompilerParams(vmem_limit_bytes=VMEM_BYTES), name="finish_frames",
        )(mine, other, my_sum)
        theirs = swap_tok(mine, 1)
        their_sum = swap_tok(my_sum, 1)
        frame_map = pl.pallas_call(
            place_frames, in_specs=[SMEM, VMEM, VMEM], out_specs=ANY, out_shape=jax.ShapeDtypeStruct((nf, d), BF16),
            scratch_shapes=[pltpu.SemaphoreType.DMA((2,))], name="place_frames",
        )(core.reshape(1).astype(jnp.int32), mine, theirs)
        low = jnp.where(core == 0, my_sum, their_sum)
        high = jnp.where(core == 0, their_sum, my_sum)
        row_sum = jnp.concatenate([low, high], axis=1)[0]
        mass_ratio = row_sum / (frame_mass / frame_total)
    return frame_map, token_map, mass_ratio


def solution(mesh):
    return jax.shard_map(
        shards,
        mesh=mesh,
        in_specs=(P("ctx", None), P("tok", None), P("ctx"), P("tok")),
        out_specs=(P("ctx", None), P("tok", None), P("ctx")),
        check_vma=False,
    )
```

```python
import functools
import math

import jax
import jax.numpy as jnp
from jax import lax
from jax.experimental import pallas as pl
from jax.experimental.pallas import tpu as pltpu
from jax.sharding import PartitionSpec as P

F32, BF16 = jnp.float32, jnp.bfloat16
W = 256
TOK = 256
CHUNK = 128
SPLIT = 4
SHARES = (2, 3, 3)
HELD = 4
PAIR = 1
EXTRA = 256
ORDER = ((16, 2), (1, 4), (4, 4))
VMEM_BYTES = 20 * 1024 * 1024
VMEM = pl.BlockSpec(memory_space=pltpu.VMEM)
SMEM = pl.BlockSpec(memory_space=pltpu.SMEM)
ANY = pl.BlockSpec(memory_space=pl.ANY)


def swap_tok(value, bit):
    return lax.ppermute(value, "tok", [(i, i ^ bit) for i in range(lax.axis_size("tok"))])


def shift(value, stride, step, size):
    pairs = []
    for i in range(lax.axis_size("ctx")):
        c = i // stride % size
        pairs.append((i, i + ((c + step) % size - c) * stride))
    return lax.ppermute(value, "ctx", pairs)


def log2(x):
    return jnp.log(x) * (1.0 / math.log(2.0))


def column(row, out_ref):
    for start in range(0, row.shape[1], 128):
        block = jnp.broadcast_to(row[:, start : start + 128], (128, 128))
        out_ref[start : start + 128, :] = block.T


def wide(col, width):
    return jnp.concatenate([col] * (width // 128), axis=1)


def merge_lse(parts):
    highest = functools.reduce(jnp.maximum, parts)
    return highest + log2(sum(jnp.exp2(part - highest) for part in parts))


def ring(value, stride, size):
    return [value] + [shift(value, stride, step, size) for step in range(1, size)]


def row_slice(i, size):
    return pl.ds(pl.multiple_of(i * size, size), size)


def turn(in_ref, out_ref):
    out_ref[...] = in_ref[...].T


def first_rows(scale, *refs):
    t_refs, (f_ref, lse_ref, s_ref) = refs[:SPLIT], refs[SPLIT:]
    i = pl.program_id(0)
    tokens = jnp.concatenate([t_ref[...] for t_ref in t_refs])
    product = lax.dot_general(tokens, f_ref[...], (((1,), (1,)), ((), ())), preferred_element_type=F32) * scale
    count = f_ref.shape[0] // W
    for n in range(count):
        s_ref[i * count + n] = product[:, n * W : (n + 1) * W]
    for n in range(count):
        highest = total = None
        for c in range(0, tokens.shape[0], CHUNK):
            s = s_ref[i * count + n, c : c + CHUNK, :].reshape(CHUNK // 8, 8, W)
            top = jnp.max(s, axis=0)
            if highest is None:
                highest = top
                total = jnp.sum(jnp.exp2(s - highest[None]), axis=0)
            else:
                top = jnp.maximum(highest, top)
                total = total * jnp.exp2(highest - top) + jnp.sum(jnp.exp2(s - top[None]), axis=0)
                highest = top
        top = jnp.max(highest, axis=0, keepdims=True)
        lse = top + log2(jnp.sum(total * jnp.exp2(highest - top), axis=0, keepdims=True))
        lse_ref[:, n * W : (n + 1) * W] = lse


def first_cols(s_ref, all_ref, fm_ref, lse_ref, u_ref, mass_ref):
    i = pl.program_id(0)

    @pl.when(i == 0)
    def _():
        u_ref[...] = log2(fm_ref[...]) - all_ref[...]
        mass_ref[...] = jnp.broadcast_to(jnp.sum(fm_ref[...]).reshape(1, 1), (1, 128))

    step = 16
    found = []
    for r in range(0, TOK, step):
        rows = pl.ds(pl.multiple_of(i * TOK + r, step), step)
        tiles = [
            s_ref[c, rows, w : w + 128] + u_ref[:, c * W + w : c * W + w + 128]
            for c in range(s_ref.shape[0])
            for w in range(0, W, 128)
        ]
        highest = functools.reduce(jnp.maximum, tiles)
        total = sum(jnp.exp2(tile - highest) for tile in tiles)
        top = jnp.max(highest, axis=1, keepdims=True)
        lse = top + log2(jnp.sum(total * jnp.exp2(highest - top), axis=1, keepdims=True))
        found.append(jnp.broadcast_to(lse, (step, 128)))
    lse_ref[...] = jnp.concatenate(found).T[0:1]


def second_rows(s_ref, all_ref, tm_ref, u_ref, sum_ref, e_ref, col_ref):
    i = pl.program_id(0)
    nt = s_ref.shape[1]
    nf = u_ref.shape[1]

    @pl.when(i == 0)
    def _():
        column(log2(tm_ref[...]) - all_ref[...], col_ref)
        sum_ref[:, nf:] = jnp.broadcast_to(jnp.sum(tm_ref[...]).reshape(1, 1), (1, EXTRA))

    u = u_ref[:, row_slice(i, W)]
    total = None
    for c in range(0, nt, CHUNK):
        e = jnp.exp2(s_ref[i, c : c + CHUNK, :] + wide(col_ref[c : c + CHUNK, :], W) + u)
        e_ref[i, c : c + CHUNK, :] = e
        part = jnp.sum(e.reshape(CHUNK // 8, 8, W), axis=0)
        total = part if total is None else total + part
    sum_ref[:, row_slice(i, W)] = jnp.sum(total, axis=0, keepdims=True)


def col_sums(e_ref, total_ref, fm_ref, sum_ref, alpha_ref, share_ref):
    i = pl.program_id(0)
    nf = fm_ref.shape[1]

    @pl.when(i == 0)
    def _():
        alpha = fm_ref[...] / total_ref[:, :nf]
        alpha_ref[...] = alpha
        share_ref[...] = alpha / wide(total_ref[:, nf : nf + 128], nf)

    step = 64
    found = []
    for r in range(0, TOK, step):
        rows = pl.ds(pl.multiple_of(i * TOK + r, step), step)
        total = None
        for c in range(e_ref.shape[0]):
            p = e_ref[c, rows, :] * alpha_ref[:, c * W : (c + 1) * W]
            for w in range(0, W, 128):
                part = p[:, w : w + 128]
                total = part if total is None else total + part
        found.append(total)
    sum_ref[...] = jnp.sum(jnp.concatenate(found).T, axis=0, keepdims=True)


def token_parts(first, e_ref, alpha_ref, f_ref, *refs):
    out_ref, stored_ref, sems = refs[-3:]
    i = pl.program_id(0)

    def store(step):
        some = row_slice(first + step, TOK)
        return pltpu.make_async_copy(e_ref.at[:, some, :], stored_ref.at[:, some, :], sems.at[step])

    store(i).start()
    rows = row_slice(first + i, TOK)
    acc = None
    for c in range(e_ref.shape[0]):
        p = (e_ref[c, rows, :] * alpha_ref[:, c * W : (c + 1) * W]).astype(BF16)
        part = jnp.dot(p, f_ref[c * W : (c + 1) * W, :], preferred_element_type=F32)
        acc = part if acc is None else acc + part
    out_ref[...] = acc.astype(BF16)

    @pl.when(i == pl.num_programs(0) - 1)
    def _():
        for step in range(sems.shape[0]):
            store(step).wait()


def frame_parts(
    base_ref, e_ref, total_ref, tm_ref, share_ref, turned_ref, sum_ref, theirs_ref, mine_ref,
    col_ref, held_ref, tt_ref, sems, tt_sem,
):
    i = pl.program_id(0)
    slabs = pl.num_programs(0)

    def fetch(k):
        slot = lax.rem(k, HELD)
        return pltpu.make_async_copy(e_ref.at[lax.rem(base_ref[0] + k, slabs)], held_ref.at[slot], sems.at[slot])

    @pl.when(i == 0)
    def _():
        fetch(0).start()
        copy = pltpu.make_async_copy(turned_ref, tt_ref, tt_sem)
        copy.start()
        for k in range(1, HELD - 1):
            fetch(k).start()
        column(tm_ref[...] / total_ref[...], col_ref)
        copy.wait()

    @pl.when(i + HELD - 1 < slabs)
    def _():
        fetch(i + HELD - 1).start()

    fetch(i).wait()
    share = share_ref[:, row_slice(lax.rem(base_ref[0] + i, slabs), W)]
    p = held_ref[lax.rem(i, HELD)] * wide(col_ref[...], W) * share
    sum_ref[...] = jnp.sum(p, axis=0, keepdims=True)
    block = jnp.dot(tt_ref[...], p.astype(BF16), preferred_element_type=F32).T.astype(BF16)

    @pl.when(i < slabs // 2)
    def _():
        theirs_ref[...] = block

    @pl.when(i >= slabs // 2)
    def _():
        mine_ref[...] = block


def sum_pieces(*refs):
    out_ref = refs[-1]
    rows = refs[0].shape[1]
    for k, pieces_ref in enumerate(refs[:-1]):
        acc = pieces_ref[0].astype(F32)
        for n in range(1, pieces_ref.shape[0]):
            acc = acc + pieces_ref[n].astype(F32)
        out_ref[k * rows : (k + 1) * rows, :] = acc.astype(BF16)


def finish_pieces(mine_ref, other_ref, total_ref, out_ref, col_ref, done_ref, sems):
    column(total_ref[...], col_ref)
    d = mine_ref.shape[1]
    done = (mine_ref[...].astype(F32) + other_ref[...].astype(F32)) / wide(col_ref[...], d)
    done_ref[...] = done.astype(BF16)
    copies = [pltpu.make_async_copy(done_ref, out_ref.at[k], sems.at[k]) for k in range(out_ref.shape[0])]
    for copy in copies:
        copy.start()
    for copy in copies:
        copy.wait()


def place_tokens(pieces_ref, out_ref, held_ref, sems, out_sems):
    count, rows = pieces_ref.shape[0], pieces_ref.shape[1]
    ins = [pltpu.make_async_copy(pieces_ref.at[k], held_ref.at[k], sems.at[k]) for k in range(count)]
    outs = [
        pltpu.make_async_copy(held_ref.at[k], out_ref.at[k * rows : (k + 1) * rows, :], out_sems.at[k])
        for k in range(count)
    ]
    for copy in ins:
        copy.start()
    for k in range(count):
        ins[k].wait()
        outs[k].start()
    for copy in outs:
        copy.wait()


def finish_frames(core_ref, mine_ref, other_ref, total_ref, out_ref, map_ref, col_ref, sem):
    column(total_ref[...], col_ref)
    rows, d = mine_ref.shape
    for r in range(0, rows, 128):
        some = slice(r, r + 128)
        done = (mine_ref[some, :].astype(F32) + other_ref[some, :].astype(F32)) / wide(col_ref[some, :], d)
        out_ref[some, :] = done.astype(BF16)
    copy = pltpu.make_async_copy(out_ref, map_ref.at[row_slice(core_ref[0], rows), :], sem)
    copy.start()
    copy.wait()


def place_frames(core_ref, theirs_ref, half_ref, map_ref, sem):
    rows = theirs_ref.shape[0]
    copy = pltpu.make_async_copy(theirs_ref, map_ref.at[row_slice(1 - core_ref[0], rows), :], sem)
    copy.start()
    copy.wait()


def whole(*shape):
    return pl.BlockSpec(shape, lambda i: (0,) * len(shape))


def rows(size, width):
    return pl.BlockSpec((size, width), lambda i: (i, 0))


def lanes(size):
    return pl.BlockSpec((1, size), lambda i: (0, i))


def f32(*shape):
    return jax.ShapeDtypeStruct(shape, F32)


def call(body, steps, in_specs, out_specs, out_shape, scratch=(), **kwargs):
    return pl.pallas_call(
        body,
        grid=(steps,),
        in_specs=in_specs,
        out_specs=out_specs,
        out_shape=out_shape,
        scratch_shapes=scratch,
        compiler_params=pltpu.CompilerParams(vmem_limit_bytes=VMEM_BYTES),
        **kwargs,
    )


def shards(frames, tokens, frame_mass, token_mass):
    nf, d = frames.shape
    nt = tokens.shape[0]
    n_ctx = lax.axis_size("ctx")
    scale = math.log2(math.e) / math.sqrt(d)
    fm, tm = frame_mass.reshape(1, nf), token_mass.reshape(1, nt)
    slabs, steps = nf // W, nt // TOK
    kept = pltpu.VMEM((slabs, nt, W), F32)
    ctx, core = lax.axis_index("ctx"), lax.axis_index("tok") % 2
    hbm = pl.BlockSpec(memory_space=pltpu.HBM)

    lse, s = call(
        functools.partial(first_rows, scale), slabs // PAIR,
        [pl.BlockSpec((nt // SPLIT, d), lambda i, k=k: (k, 0)) for k in range(SPLIT)] + [rows(PAIR * W, d)],
        [lanes(PAIR * W), VMEM], [f32(1, nf), kept], name="first_rows",
    )(*[pltpu.with_memory_space_constraint(tokens, pltpu.HBM)] * SPLIT, pltpu.with_memory_space_constraint(frames, pltpu.HBM))
    with jax.named_scope("rows_one"):
        lse = merge_lse([lse, swap_tok(lse, 1)])
        lse = merge_lse([lse, swap_tok(lse, 2)])
    lse, u, frame_total = call(
        first_cols, steps, [VMEM, whole(1, nf), whole(1, nf)], [lanes(TOK), whole(1, nf), whole(1, 128)],
        [f32(1, nt), f32(1, nf), f32(1, 128)], name="first_cols",
    )(s, lse, fm)
    with jax.named_scope("cols_one"):
        lse = jnp.concatenate([lse, frame_total], axis=1)
        parts = lax.all_to_all(jnp.broadcast_to(lse[None], (n_ctx, 1, nt + 128)), "ctx", 0, 0)[:, 0]
        highest = jnp.max(parts[:, :nt], axis=0, keepdims=True)
        lse = highest + log2(jnp.sum(jnp.exp2(parts[:, :nt] - highest), axis=0, keepdims=True))
        frame_total = jnp.sum(parts[:, nt])
    part, e = call(
        second_rows, slabs, [VMEM, whole(1, nt), whole(1, nt), whole(1, nf)], [whole(1, nf + EXTRA), VMEM],
        [f32(1, nf + EXTRA), kept], [pltpu.VMEM((nt, 128), F32)], input_output_aliases={0: 1}, name="second_rows",
    )(s, lse, tm, u)
    with jax.named_scope("rows_two"):
        part = part + swap_tok(part, 1)
        tokens_later, part = lax.optimization_barrier((tokens, part))
        turned = call(
            turn, 4, [rows(nt // 4, d)], pl.BlockSpec((d, nt // 4), lambda i: (0, i)),
            pltpu.HBM((d, nt), BF16), name="turn",
        )(tokens_later)
        part = part + swap_tok(part, 2)
        part, turned = lax.optimization_barrier((part, turned))
    part, alpha, share = call(
        col_sums, steps, [VMEM, whole(1, nf + EXTRA), whole(1, nf)], [lanes(TOK), whole(1, nf), whole(1, nf)],
        [f32(1, nt), f32(1, nf), f32(1, nf)], name="col_sums",
    )(e, part, fm)

    def some_token_parts(first, count, held):
        return call(
            functools.partial(token_parts, first), count, [VMEM, whole(1, nf), whole(nf, d)] + [hbm] * len(held),
            [pl.BlockSpec((TOK, d), lambda i: (first + i, 0)), hbm],
            [pltpu.HBM((nt, d), BF16), pltpu.HBM((slabs, nt, W), F32)], [pltpu.SemaphoreType.DMA((count,))],
            input_output_aliases={3 + k: k for k in range(len(held))}, name="token_parts",
        )(e, alpha, frames, *held)

    with jax.named_scope("cols_two"):
        held, first = [], 0
        col_total = part
        for (stride, size), count in zip(ORDER, SHARES):
            held = list(some_token_parts(first, count, held))
            first += count
            col_total = sum(ring(col_total, stride, size))
            col_total, held[0] = lax.optimization_barrier((col_total, held[0]))
        token_part, e = held
    with jax.named_scope("token_scatter"):
        plane, own = 16, nt // 16
        planes = [list(range(z, z + plane)) for z in range(0, n_ctx, plane)]
        pieces = lax.all_to_all(token_part.reshape(plane, own, d), "ctx", 0, 0, axis_index_groups=planes)
    e = pltpu.with_memory_space_constraint(e, pltpu.HBM)
    half = slabs // 2
    base = ((1 - core) * half).reshape(1).astype(jnp.int32)
    with jax.named_scope("frame_rows"):
        sums, theirs, mine = pl.pallas_call(
            frame_parts,
            grid=(slabs,),
            in_specs=[SMEM, hbm, whole(1, nt), whole(1, nt), whole(1, nf), hbm],
            out_specs=[
                lanes(W),
                pl.BlockSpec((W, d), lambda i: (jnp.minimum(i, half - 1), 0)),
                pl.BlockSpec((W, d), lambda i: (jnp.maximum(i - half, 0), 0)),
            ],
            out_shape=[f32(1, nf)] + [jax.ShapeDtypeStruct((nf // 2, d), BF16)] * 2,
            scratch_shapes=[
                pltpu.VMEM((nt, 128), F32),
                pltpu.VMEM((HELD, nt, W), F32),
                pltpu.VMEM((d, nt), BF16),
                pltpu.SemaphoreType.DMA((HELD,)),
                pltpu.SemaphoreType.DMA,
            ],
            compiler_params=pltpu.CompilerParams(vmem_limit_bytes=VMEM_BYTES),
            name="frame_parts",
        )(base, e, col_total, tm, share, pltpu.with_memory_space_constraint(turned, pltpu.HBM))
        my_sum = sums[:, nf // 2 :] + swap_tok(sums[:, : nf // 2], 1)
        other_sum = swap_tok(my_sum, 2)
        mine = (mine.astype(F32) + swap_tok(theirs, 1).astype(F32)).astype(BF16)
    with jax.named_scope("token_sums"):
        pieces, mine, other_sum = lax.optimization_barrier((pieces, mine, other_sum))
        deal = own // (2 * SPLIT)
        piece = call(
            sum_pieces, 2,
            [pl.BlockSpec((plane, deal, d), lambda i, k=k: (0, i * SPLIT + k, 0)) for k in range(SPLIT)],
            rows(own // 2, d), jax.ShapeDtypeStruct((own, d), BF16), name="sum_pieces",
        )(*[pieces] * SPLIT)
        other_piece = shift(piece, 16, 1, 2)

    with jax.named_scope("token_gather"):
        col_mine = lax.dynamic_slice_in_dim(col_total, ctx % plane * own, own, axis=1)
        pieces = pl.pallas_call(
            finish_pieces, in_specs=[VMEM] * 3, out_specs=hbm, out_shape=pltpu.HBM((plane, own, d), BF16),
            scratch_shapes=[
                pltpu.VMEM((own, 128), F32),
                pltpu.VMEM((own, d), BF16),
                pltpu.SemaphoreType.DMA((plane,)),
            ],
            compiler_params=pltpu.CompilerParams(vmem_limit_bytes=VMEM_BYTES), name="finish_pieces",
        )(piece, other_piece, col_mine)
        mine, pieces = lax.optimization_barrier((mine, pieces))
        other = swap_tok(mine, 2)
        pieces = lax.all_to_all(pieces, "ctx", 0, 0, axis_index_groups=planes)
    with jax.named_scope("frame_sums"):
        my_sum = my_sum + other_sum
        their_sum = swap_tok(my_sum, 1)
        low = jnp.where(core == 0, my_sum, their_sum)
        high = jnp.where(core == 0, their_sum, my_sum)
        row_sum = jnp.concatenate([low, high], axis=1)[0]
        mass_ratio = row_sum / (frame_mass / frame_total)
        other, mass_ratio = lax.optimization_barrier((other, mass_ratio))
    with jax.named_scope("frame_out"):
        which = core.reshape(1).astype(jnp.int32)
        mine, frame_map = pl.pallas_call(
            finish_frames, in_specs=[SMEM] + [VMEM] * 3, out_specs=[VMEM, hbm],
            out_shape=[jax.ShapeDtypeStruct((nf // 2, d), BF16), pltpu.HBM((nf, d), BF16)],
            scratch_shapes=[pltpu.VMEM((nf // 2, 128), F32), pltpu.SemaphoreType.DMA],
            compiler_params=pltpu.CompilerParams(vmem_limit_bytes=VMEM_BYTES), name="finish_frames",
        )(which, mine, other, my_sum)
        frame_map = pl.pallas_call(
            place_frames, in_specs=[SMEM, VMEM, hbm], out_specs=hbm, out_shape=pltpu.HBM((nf, d), BF16),
            scratch_shapes=[pltpu.SemaphoreType.DMA], input_output_aliases={2: 0}, name="place_frames",
        )(which, swap_tok(mine, 1), frame_map)
        pieces, frame_map = lax.optimization_barrier((pieces, frame_map))
        token_map = pl.pallas_call(
            place_tokens, in_specs=[hbm], out_specs=hbm, out_shape=pltpu.HBM((nt, d), BF16),
            scratch_shapes=[
                pltpu.VMEM((plane, own, d), BF16),
                pltpu.SemaphoreType.DMA((plane,)),
                pltpu.SemaphoreType.DMA((plane,)),
            ],
            compiler_params=pltpu.CompilerParams(vmem_limit_bytes=VMEM_BYTES), name="place_tokens",
        )(pltpu.with_memory_space_constraint(pieces, pltpu.HBM))
    return frame_map, token_map, mass_ratio


def solution(mesh):
    return jax.shard_map(
        shards,
        mesh=mesh,
        in_specs=(P("ctx", None), P("tok", None), P("ctx"), P("tok")),
        out_specs=(P("ctx", None), P("tok", None), P("ctx")),
        check_vma=False,
    )
```

```python
import functools
import math

import jax
import jax.numpy as jnp
from jax import lax
from jax.experimental import pallas as pl
from jax.experimental.pallas import tpu as pltpu
from jax.sharding import PartitionSpec as P

F32, BF16 = jnp.float32, jnp.bfloat16
W = 256
TOK = 256
CHUNK = 128
SPLIT = 4
STAGES = ((16, 2, 0, 2), (1, 4, 0, 1), (1, 4, 1, 2), (4, 4, 0, 1), (4, 4, 1, 2))
EARLY = 4
HELD = 4
PAIR = 1
EXTRA = 256
VMEM_BYTES = 20 * 1024 * 1024
VMEM = pl.BlockSpec(memory_space=pltpu.VMEM)
SMEM = pl.BlockSpec(memory_space=pltpu.SMEM)
ANY = pl.BlockSpec(memory_space=pl.ANY)


def swap_tok(value, bit):
    return lax.ppermute(value, "tok", [(i, i ^ bit) for i in range(lax.axis_size("tok"))])


def meet(value, stride, size, later):
    pairs = []
    for i in range(lax.axis_size("ctx")):
        c = i // stride % size
        other = c + 1 if c % 2 == later else c - 1
        pairs.append((i, i + (other % size - c) * stride))
    return lax.ppermute(value, "ctx", pairs)


def log2(x):
    return jnp.log(x) * (1.0 / math.log(2.0))


def column(row, out_ref):
    for start in range(0, row.shape[1], 128):
        block = jnp.broadcast_to(row[:, start : start + 128], (128, 128))
        out_ref[start : start + 128, :] = block.T


def wide(col, width):
    return jnp.concatenate([col] * (width // 128), axis=1)


def merge_lse(parts):
    highest = functools.reduce(jnp.maximum, parts)
    return highest + log2(sum(jnp.exp2(part - highest) for part in parts))


def row_slice(i, size):
    return pl.ds(pl.multiple_of(i * size, size), size)


def turn(in_ref, out_ref):
    out_ref[...] = in_ref[...].T


def first_rows(scale, *refs):
    t_refs, (f_ref, lse_ref, s_ref) = refs[:SPLIT], refs[SPLIT:]
    i = pl.program_id(0)
    tokens = jnp.concatenate([t_ref[...] for t_ref in t_refs])
    product = lax.dot_general(tokens, f_ref[...], (((1,), (1,)), ((), ())), preferred_element_type=F32) * scale
    count = f_ref.shape[0] // W
    for n in range(count):
        s_ref[i * count + n] = product[:, n * W : (n + 1) * W]
    for n in range(count):
        highest = total = None
        for c in range(0, tokens.shape[0], CHUNK):
            s = s_ref[i * count + n, c : c + CHUNK, :].reshape(CHUNK // 8, 8, W)
            top = jnp.max(s, axis=0)
            if highest is None:
                highest = top
                total = jnp.sum(jnp.exp2(s - highest[None]), axis=0)
            else:
                top = jnp.maximum(highest, top)
                total = total * jnp.exp2(highest - top) + jnp.sum(jnp.exp2(s - top[None]), axis=0)
                highest = top
        top = jnp.max(highest, axis=0, keepdims=True)
        lse = top + log2(jnp.sum(total * jnp.exp2(highest - top), axis=0, keepdims=True))
        lse_ref[:, n * W : (n + 1) * W] = lse


def first_cols(s_ref, all_ref, fm_ref, lse_ref, u_ref, mass_ref):
    i = pl.program_id(0)

    @pl.when(i == 0)
    def _():
        u_ref[...] = log2(fm_ref[...]) - all_ref[...]
        mass_ref[...] = jnp.broadcast_to(jnp.sum(fm_ref[...]).reshape(1, 1), (1, 128))

    step = 16
    found = []
    for r in range(0, TOK, step):
        rows = pl.ds(pl.multiple_of(i * TOK + r, step), step)
        tiles = [
            s_ref[c, rows, w : w + 128] + u_ref[:, c * W + w : c * W + w + 128]
            for c in range(s_ref.shape[0])
            for w in range(0, W, 128)
        ]
        highest = functools.reduce(jnp.maximum, tiles)
        total = sum(jnp.exp2(tile - highest) for tile in tiles)
        top = jnp.max(highest, axis=1, keepdims=True)
        lse = top + log2(jnp.sum(total * jnp.exp2(highest - top), axis=1, keepdims=True))
        found.append(jnp.broadcast_to(lse, (step, 128)))
    lse_ref[...] = jnp.concatenate(found).T[0:1]


def store(e_ref, stored_ref, sems, slabs):
    size = e_ref.shape[1] // SPLIT
    return [
        pltpu.make_async_copy(
            e_ref.at[slab, pl.ds(k * size, size), :], stored_ref.at[slab, pl.ds(k * size, size), :], sems.at[n, k]
        )
        for n, slab in enumerate(slabs)
        for k in range(SPLIT)
    ]


def during(copies):
    @pl.when(pl.program_id(0) == 0)
    def _():
        for copy in copies:
            copy.start()

    def finish():
        @pl.when(pl.program_id(0) == pl.num_programs(0) - 1)
        def _():
            for copy in copies:
                copy.wait()

    return finish


def second_rows(s_ref, all_ref, tm_ref, u_ref, sum_ref, e_ref, stored_ref, col_ref, sems):
    i = pl.program_id(0)
    nt = s_ref.shape[1]
    nf = u_ref.shape[1]

    @pl.when(i == 0)
    def _():
        column(log2(tm_ref[...]) - all_ref[...], col_ref)
        sum_ref[:, nf:] = jnp.broadcast_to(jnp.sum(tm_ref[...]).reshape(1, 1), (1, EXTRA))

    u = u_ref[:, row_slice(i, W)]
    total = None
    for c in range(0, nt, CHUNK):
        e = jnp.exp2(s_ref[i, c : c + CHUNK, :] + wide(col_ref[c : c + CHUNK, :], W) + u)
        e_ref[i, c : c + CHUNK, :] = e
        part = jnp.sum(e.reshape(CHUNK // 8, 8, W), axis=0)
        total = part if total is None else total + part
    sum_ref[:, row_slice(i, W)] = jnp.sum(total, axis=0, keepdims=True)
    copies = store(e_ref, stored_ref, sems, range(EARLY))
    for slab in range(EARLY):

        @pl.when(i == slab)
        def _(slab=slab):
            for copy in copies[slab * SPLIT : (slab + 1) * SPLIT]:
                copy.start()

    @pl.when(i == pl.num_programs(0) - 1)
    def _():
        for copy in copies:
            copy.wait()


def col_sums(e_ref, total_ref, fm_ref, held_ref, sum_ref, alpha_ref, share_ref, stored_ref, sems):
    i = pl.program_id(0)
    nf = fm_ref.shape[1]
    finish = during(store(e_ref, stored_ref, sems, range(EARLY, EARLY + 2)))

    @pl.when(i == 0)
    def _():
        alpha = fm_ref[...] / total_ref[:, :nf]
        alpha_ref[...] = alpha
        share_ref[...] = alpha / wide(total_ref[:, nf : nf + 128], nf)

    step = 64
    found = []
    for r in range(0, TOK, step):
        rows = pl.ds(pl.multiple_of(i * TOK + r, step), step)
        total = None
        for c in range(e_ref.shape[0]):
            p = e_ref[c, rows, :] * alpha_ref[:, c * W : (c + 1) * W]
            for w in range(0, W, 128):
                part = p[:, w : w + 128]
                total = part if total is None else total + part
        found.append(total)
    sum_ref[...] = jnp.sum(jnp.concatenate(found).T, axis=0, keepdims=True)
    finish()


def token_parts(first, slabs, e_ref, alpha_ref, f_ref, *refs):
    out_ref, stored_ref, sems = refs[-3:]
    finish = during(store(e_ref, stored_ref, sems, slabs))
    rows = row_slice(first + pl.program_id(0), TOK)
    acc = None
    for c in range(e_ref.shape[0]):
        p = (e_ref[c, rows, :] * alpha_ref[:, c * W : (c + 1) * W]).astype(BF16)
        part = jnp.dot(p, f_ref[c * W : (c + 1) * W, :], preferred_element_type=F32)
        acc = part if acc is None else acc + part
    out_ref[...] = acc.astype(BF16)
    finish()


def frame_parts(
    base_ref, e_ref, total_ref, tm_ref, share_ref, turned_ref, sum_ref, theirs_ref, mine_ref,
    col_ref, held_ref, tt_ref, sems, tt_sem,
):
    i = pl.program_id(0)
    slabs = pl.num_programs(0)

    def fetch(k):
        slot = lax.rem(k, HELD)
        return pltpu.make_async_copy(e_ref.at[lax.rem(base_ref[0] + k, slabs)], held_ref.at[slot], sems.at[slot])

    @pl.when(i == 0)
    def _():
        fetch(0).start()
        copy = pltpu.make_async_copy(turned_ref, tt_ref, tt_sem)
        copy.start()
        for k in range(1, HELD - 1):
            fetch(k).start()
        column(tm_ref[...] / total_ref[...], col_ref)
        copy.wait()

    @pl.when(i + HELD - 1 < slabs)
    def _():
        fetch(i + HELD - 1).start()

    fetch(i).wait()
    share = share_ref[:, row_slice(lax.rem(base_ref[0] + i, slabs), W)]
    p = held_ref[lax.rem(i, HELD)] * wide(col_ref[...], W) * share
    sum_ref[...] = jnp.sum(p, axis=0, keepdims=True)
    block = jnp.dot(tt_ref[...], p.astype(BF16), preferred_element_type=F32).T.astype(BF16)

    @pl.when(i < slabs // 2)
    def _():
        theirs_ref[...] = block

    @pl.when(i >= slabs // 2)
    def _():
        mine_ref[...] = block


def sum_pieces(*refs):
    out_ref = refs[-1]
    rows = refs[0].shape[1]
    for k, pieces_ref in enumerate(refs[:-1]):
        acc = pieces_ref[0].astype(F32)
        for n in range(1, pieces_ref.shape[0]):
            acc = acc + pieces_ref[n].astype(F32)
        out_ref[k * rows : (k + 1) * rows, :] = acc.astype(BF16)


def finish_pieces(mine_ref, other_ref, total_ref, out_ref, col_ref, done_ref, sems):
    column(total_ref[...], col_ref)
    d = mine_ref.shape[1]
    done = (mine_ref[...].astype(F32) + other_ref[...].astype(F32)) / wide(col_ref[...], d)
    done_ref[...] = done.astype(BF16)
    copies = [pltpu.make_async_copy(done_ref, out_ref.at[k], sems.at[k]) for k in range(out_ref.shape[0])]
    for copy in copies:
        copy.start()
    for copy in copies:
        copy.wait()


def place_tokens(pieces_ref, out_ref, held_ref, sems, out_sems):
    count, rows = pieces_ref.shape[0], pieces_ref.shape[1]
    ins = [pltpu.make_async_copy(pieces_ref.at[k], held_ref.at[k], sems.at[k]) for k in range(count)]
    outs = [
        pltpu.make_async_copy(held_ref.at[k], out_ref.at[k * rows : (k + 1) * rows, :], out_sems.at[k])
        for k in range(count)
    ]
    for copy in ins:
        copy.start()
    for k in range(count):
        ins[k].wait()
        outs[k].start()
    for copy in outs:
        copy.wait()


def finish_frames(core_ref, mine_ref, other_ref, total_ref, out_ref, map_ref, col_ref, sem):
    column(total_ref[...], col_ref)
    rows, d = mine_ref.shape
    for r in range(0, rows, 128):
        some = slice(r, r + 128)
        done = (mine_ref[some, :].astype(F32) + other_ref[some, :].astype(F32)) / wide(col_ref[some, :], d)
        out_ref[some, :] = done.astype(BF16)
    copy = pltpu.make_async_copy(out_ref, map_ref.at[row_slice(core_ref[0], rows), :], sem)
    copy.start()
    copy.wait()


def place_frames(core_ref, theirs_ref, half_ref, map_ref, sem):
    rows = theirs_ref.shape[0]
    copy = pltpu.make_async_copy(theirs_ref, map_ref.at[row_slice(1 - core_ref[0], rows), :], sem)
    copy.start()
    copy.wait()


def whole(*shape):
    return pl.BlockSpec(shape, lambda i: (0,) * len(shape))


def rows(size, width):
    return pl.BlockSpec((size, width), lambda i: (i, 0))


def lanes(size):
    return pl.BlockSpec((1, size), lambda i: (0, i))


def f32(*shape):
    return jax.ShapeDtypeStruct(shape, F32)


def call(body, steps, in_specs, out_specs, out_shape, scratch=(), **kwargs):
    return pl.pallas_call(
        body,
        grid=(steps,),
        in_specs=in_specs,
        out_specs=out_specs,
        out_shape=out_shape,
        scratch_shapes=scratch,
        compiler_params=pltpu.CompilerParams(vmem_limit_bytes=VMEM_BYTES),
        **kwargs,
    )


def shards(frames, tokens, frame_mass, token_mass):
    nf, d = frames.shape
    nt = tokens.shape[0]
    n_ctx = lax.axis_size("ctx")
    scale = math.log2(math.e) / math.sqrt(d)
    fm, tm = frame_mass.reshape(1, nf), token_mass.reshape(1, nt)
    slabs, steps = nf // W, nt // TOK
    kept = pltpu.VMEM((slabs, nt, W), F32)
    ctx, core = lax.axis_index("ctx"), lax.axis_index("tok") % 2
    hbm = pl.BlockSpec(memory_space=pltpu.HBM)

    lse, s = call(
        functools.partial(first_rows, scale), slabs // PAIR,
        [pl.BlockSpec((nt // SPLIT, d), lambda i, k=k: (k, 0)) for k in range(SPLIT)] + [rows(PAIR * W, d)],
        [lanes(PAIR * W), VMEM], [f32(1, nf), kept], name="first_rows",
    )(*[pltpu.with_memory_space_constraint(tokens, pltpu.HBM)] * SPLIT, pltpu.with_memory_space_constraint(frames, pltpu.HBM))
    with jax.named_scope("rows_one"):
        lse = merge_lse([lse, swap_tok(lse, 1)])
        lse = merge_lse([lse, swap_tok(lse, 2)])
    lse, u, frame_total = call(
        first_cols, steps, [VMEM, whole(1, nf), whole(1, nf)], [lanes(TOK), whole(1, nf), whole(1, 128)],
        [f32(1, nt), f32(1, nf), f32(1, 128)], name="first_cols",
    )(s, lse, fm)
    with jax.named_scope("cols_one"):
        lse = jnp.concatenate([lse, frame_total], axis=1)
        parts = lax.all_to_all(jnp.broadcast_to(lse[None], (n_ctx, 1, nt + 128)), "ctx", 0, 0)[:, 0]
        highest = jnp.max(parts[:, :nt], axis=0, keepdims=True)
        lse = highest + log2(jnp.sum(jnp.exp2(parts[:, :nt] - highest), axis=0, keepdims=True))
        frame_total = jnp.sum(parts[:, nt])
    part, e, stored = call(
        second_rows, slabs, [VMEM, whole(1, nt), whole(1, nt), whole(1, nf)], [whole(1, nf + EXTRA), VMEM, hbm],
        [f32(1, nf + EXTRA), kept, pltpu.HBM((slabs, nt, W), F32)],
        [pltpu.VMEM((nt, 128), F32), pltpu.SemaphoreType.DMA((EARLY, SPLIT))],
        input_output_aliases={0: 1}, name="second_rows",
    )(s, lse, tm, u)
    with jax.named_scope("rows_two"):
        part = part + swap_tok(part, 1)
        tokens_later, part = lax.optimization_barrier((tokens, part))
        turned = call(
            turn, 4, [rows(nt // 4, d)], pl.BlockSpec((d, nt // 4), lambda i: (0, i)),
            pltpu.HBM((d, nt), BF16), name="turn",
        )(tokens_later)
        part = part + swap_tok(part, 2)
        part, turned = lax.optimization_barrier((part, turned))
    part, alpha, share, stored = call(
        col_sums, steps, [VMEM, whole(1, nf + EXTRA), whole(1, nf), hbm],
        [lanes(TOK), whole(1, nf), whole(1, nf), hbm],
        [f32(1, nt), f32(1, nf), f32(1, nf), pltpu.HBM((slabs, nt, W), F32)],
        [pltpu.SemaphoreType.DMA((2, SPLIT))], input_output_aliases={3: 3}, name="col_sums",
    )(e, part, fm, stored)

    def some_token_parts(first, count, late, stored, held):
        return call(
            functools.partial(token_parts, first, late), count, [VMEM, whole(1, nf), VMEM, hbm] + [hbm] * len(held),
            [pl.BlockSpec((TOK, d), lambda i: (first + i, 0)), hbm],
            [pltpu.HBM((nt, d), BF16), pltpu.HBM((slabs, nt, W), F32)], [pltpu.SemaphoreType.DMA((1, SPLIT))],
            input_output_aliases={3: 1} | {4 + k: 0 for k in range(len(held))}, name="token_parts",
        )(e, alpha, frames, stored, *held)

    with jax.named_scope("cols_two"):
        held, first = [], 0
        late = list(range(EARLY + 2, slabs))
        col_total = part
        for stride, size, later, count in STAGES:
            which = [late.pop()] if late and count > 1 else []
            token_part, stored = some_token_parts(first, count, which, stored, held)
            first += count
            col_total = col_total + meet(col_total, stride, size, later)
            col_total, token_part = lax.optimization_barrier((col_total, token_part))
            held = [token_part]
    with jax.named_scope("token_scatter"):
        plane, own = 16, nt // 16
        planes = [list(range(z, z + plane)) for z in range(0, n_ctx, plane)]
        pieces = lax.all_to_all(token_part.reshape(plane, own, d), "ctx", 0, 0, axis_index_groups=planes)
    e = pltpu.with_memory_space_constraint(stored, pltpu.HBM)
    half = slabs // 2
    base = ((1 - core) * half).reshape(1).astype(jnp.int32)
    with jax.named_scope("frame_rows"):
        sums, theirs, mine = pl.pallas_call(
            frame_parts,
            grid=(slabs,),
            in_specs=[SMEM, hbm, whole(1, nt), whole(1, nt), whole(1, nf), hbm],
            out_specs=[
                lanes(W),
                pl.BlockSpec((W, d), lambda i: (jnp.minimum(i, half - 1), 0)),
                pl.BlockSpec((W, d), lambda i: (jnp.maximum(i - half, 0), 0)),
            ],
            out_shape=[f32(1, nf)] + [jax.ShapeDtypeStruct((nf // 2, d), BF16)] * 2,
            scratch_shapes=[
                pltpu.VMEM((nt, 128), F32),
                pltpu.VMEM((HELD, nt, W), F32),
                pltpu.VMEM((d, nt), BF16),
                pltpu.SemaphoreType.DMA((HELD,)),
                pltpu.SemaphoreType.DMA,
            ],
            compiler_params=pltpu.CompilerParams(vmem_limit_bytes=VMEM_BYTES),
            name="frame_parts",
        )(base, e, col_total, tm, share, pltpu.with_memory_space_constraint(turned, pltpu.HBM))
        my_sum = sums[:, nf // 2 :] + swap_tok(sums[:, : nf // 2], 1)
        other_sum = swap_tok(my_sum, 2)
        mine = (mine.astype(F32) + swap_tok(theirs, 1).astype(F32)).astype(BF16)
    with jax.named_scope("token_sums"):
        pieces, mine, other_sum = lax.optimization_barrier((pieces, mine, other_sum))
        deal = own // (2 * SPLIT)
        piece = call(
            sum_pieces, 2,
            [pl.BlockSpec((plane, deal, d), lambda i, k=k: (0, i * SPLIT + k, 0)) for k in range(SPLIT)],
            rows(own // 2, d), jax.ShapeDtypeStruct((own, d), BF16), name="sum_pieces",
        )(*[pieces] * SPLIT)
        other_piece = meet(piece, 16, 2, 0)
        mine, other_piece = lax.optimization_barrier((mine, other_piece))
        other = swap_tok(mine, 2)

    with jax.named_scope("token_gather"):
        col_mine = lax.dynamic_slice_in_dim(col_total, ctx % plane * own, own, axis=1)
        pieces = pl.pallas_call(
            finish_pieces, in_specs=[VMEM] * 3, out_specs=hbm, out_shape=pltpu.HBM((plane, own, d), BF16),
            scratch_shapes=[
                pltpu.VMEM((own, 128), F32),
                pltpu.VMEM((own, d), BF16),
                pltpu.SemaphoreType.DMA((plane,)),
            ],
            compiler_params=pltpu.CompilerParams(vmem_limit_bytes=VMEM_BYTES), name="finish_pieces",
        )(piece, other_piece, col_mine)
        pieces = lax.all_to_all(pieces, "ctx", 0, 0, axis_index_groups=planes)
    with jax.named_scope("frame_sums"):
        my_sum = my_sum + other_sum
        their_sum = swap_tok(my_sum, 1)
        low = jnp.where(core == 0, my_sum, their_sum)
        high = jnp.where(core == 0, their_sum, my_sum)
        row_sum = jnp.concatenate([low, high], axis=1)[0]
        mass_ratio = row_sum / (frame_mass / frame_total)
        other, mass_ratio = lax.optimization_barrier((other, mass_ratio))
    with jax.named_scope("frame_out"):
        which = core.reshape(1).astype(jnp.int32)
        mine, frame_map = pl.pallas_call(
            finish_frames, in_specs=[SMEM] + [VMEM] * 3, out_specs=[VMEM, hbm],
            out_shape=[jax.ShapeDtypeStruct((nf // 2, d), BF16), pltpu.HBM((nf, d), BF16)],
            scratch_shapes=[pltpu.VMEM((nf // 2, 128), F32), pltpu.SemaphoreType.DMA],
            compiler_params=pltpu.CompilerParams(vmem_limit_bytes=VMEM_BYTES), name="finish_frames",
        )(which, mine, other, my_sum)
        frame_map = pl.pallas_call(
            place_frames, in_specs=[SMEM, VMEM, hbm], out_specs=hbm, out_shape=pltpu.HBM((nf, d), BF16),
            scratch_shapes=[pltpu.SemaphoreType.DMA], input_output_aliases={2: 0}, name="place_frames",
        )(which, swap_tok(mine, 1), frame_map)
        pieces, frame_map = lax.optimization_barrier((pieces, frame_map))
        token_map = pl.pallas_call(
            place_tokens, in_specs=[hbm], out_specs=hbm, out_shape=pltpu.HBM((nt, d), BF16),
            scratch_shapes=[
                pltpu.VMEM((plane, own, d), BF16),
                pltpu.SemaphoreType.DMA((plane,)),
                pltpu.SemaphoreType.DMA((plane,)),
            ],
            compiler_params=pltpu.CompilerParams(vmem_limit_bytes=VMEM_BYTES), name="place_tokens",
        )(pltpu.with_memory_space_constraint(pieces, pltpu.HBM))
    return frame_map, token_map, mass_ratio


def solution(mesh):
    return jax.shard_map(
        shards,
        mesh=mesh,
        in_specs=(P("ctx", None), P("tok", None), P("ctx"), P("tok")),
        out_specs=(P("ctx", None), P("tok", None), P("ctx")),
        check_vma=False,
    )
```

```python
import functools
import math

import jax
import jax.numpy as jnp
from jax import lax
from jax.experimental import pallas as pl
from jax.experimental.pallas import tpu as pltpu
from jax.sharding import PartitionSpec as P

F32, BF16 = jnp.float32, jnp.bfloat16
W = 256
TOK = 256
CHUNK = 128
SPLIT = 4
STAGES = ((16, 2, 0, 2), (1, 4, 0, 1), (1, 4, 1, 2), (4, 4, 0, 1), (4, 4, 1, 2))
EARLY = 4
HELD = 4
PAIR = 1
EXTRA = 256
VMEM_BYTES = 20 * 1024 * 1024
VMEM = pl.BlockSpec(memory_space=pltpu.VMEM)
SMEM = pl.BlockSpec(memory_space=pltpu.SMEM)
ANY = pl.BlockSpec(memory_space=pl.ANY)


def swap_tok(value, bit):
    return lax.ppermute(value, "tok", [(i, i ^ bit) for i in range(lax.axis_size("tok"))])


def meet(value, stride, size, later):
    pairs = []
    for i in range(lax.axis_size("ctx")):
        c = i // stride % size
        other = c + 1 if c % 2 == later else c - 1
        pairs.append((i, i + (other % size - c) * stride))
    return lax.ppermute(value, "ctx", pairs)


def log2(x):
    return jnp.log(x) * (1.0 / math.log(2.0))


def column(row, out_ref):
    for start in range(0, row.shape[1], 128):
        block = jnp.broadcast_to(row[:, start : start + 128], (128, 128))
        out_ref[start : start + 128, :] = block.T


def wide(col, width):
    return jnp.concatenate([col] * (width // 128), axis=1)


def merge_lse(parts):
    highest = functools.reduce(jnp.maximum, parts)
    return highest + log2(sum(jnp.exp2(part - highest) for part in parts))


def row_slice(i, size):
    return pl.ds(pl.multiple_of(i * size, size), size)


def turn(in_ref, out_ref):
    out_ref[...] = in_ref[...].T


def first_rows(scale, *refs):
    t_refs, (f_ref, lse_ref, s_ref) = refs[:SPLIT], refs[SPLIT:]
    i = pl.program_id(0)
    tokens = jnp.concatenate([t_ref[...] for t_ref in t_refs])
    product = lax.dot_general(tokens, f_ref[...], (((1,), (1,)), ((), ())), preferred_element_type=F32) * scale
    count = f_ref.shape[0] // W
    for n in range(count):
        s_ref[i * count + n] = product[:, n * W : (n + 1) * W]
    for n in range(count):
        highest = total = None
        for c in range(0, tokens.shape[0], CHUNK):
            s = s_ref[i * count + n, c : c + CHUNK, :].reshape(CHUNK // 8, 8, W)
            top = jnp.max(s, axis=0)
            if highest is None:
                highest = top
                total = jnp.sum(jnp.exp2(s - highest[None]), axis=0)
            else:
                top = jnp.maximum(highest, top)
                total = total * jnp.exp2(highest - top) + jnp.sum(jnp.exp2(s - top[None]), axis=0)
                highest = top
        top = jnp.max(highest, axis=0, keepdims=True)
        lse = top + log2(jnp.sum(total * jnp.exp2(highest - top), axis=0, keepdims=True))
        lse_ref[:, n * W : (n + 1) * W] = lse


def first_cols(s_ref, all_ref, fm_ref, lse_ref, u_ref, mass_ref):
    i = pl.program_id(0)

    @pl.when(i == 0)
    def _():
        u_ref[...] = log2(fm_ref[...]) - all_ref[...]
        mass_ref[...] = jnp.broadcast_to(jnp.sum(fm_ref[...]).reshape(1, 1), (1, 128))

    step = 16
    found = []
    for r in range(0, TOK, step):
        rows = pl.ds(pl.multiple_of(i * TOK + r, step), step)
        tiles = [
            s_ref[c, rows, w : w + 128] + u_ref[:, c * W + w : c * W + w + 128]
            for c in range(s_ref.shape[0])
            for w in range(0, W, 128)
        ]
        highest = functools.reduce(jnp.maximum, tiles)
        total = sum(jnp.exp2(tile - highest) for tile in tiles)
        top = jnp.max(highest, axis=1, keepdims=True)
        lse = top + log2(jnp.sum(total * jnp.exp2(highest - top), axis=1, keepdims=True))
        found.append(jnp.broadcast_to(lse, (step, 128)))
    lse_ref[...] = jnp.concatenate(found).T[0:1]


def store(e_ref, stored_ref, sems, slabs):
    size = e_ref.shape[1] // SPLIT
    return [
        pltpu.make_async_copy(
            e_ref.at[slab, pl.ds(k * size, size), :], stored_ref.at[slab, pl.ds(k * size, size), :], sems.at[n, k]
        )
        for n, slab in enumerate(slabs)
        for k in range(SPLIT)
    ]


def during(copies):
    @pl.when(pl.program_id(0) == 0)
    def _():
        for copy in copies:
            copy.start()

    def finish():
        @pl.when(pl.program_id(0) == pl.num_programs(0) - 1)
        def _():
            for copy in copies:
                copy.wait()

    return finish


def second_rows(s_ref, all_ref, tm_ref, u_ref, sum_ref, e_ref, stored_ref, col_ref, sems):
    i = pl.program_id(0)
    nt = s_ref.shape[1]
    nf = u_ref.shape[1]

    @pl.when(i == 0)
    def _():
        column(log2(tm_ref[...]) - all_ref[...], col_ref)
        sum_ref[:, nf:] = jnp.broadcast_to(jnp.sum(tm_ref[...]).reshape(1, 1), (1, EXTRA))

    u = u_ref[:, row_slice(i, W)]
    total = None
    for c in range(0, nt, CHUNK):
        e = jnp.exp2(s_ref[i, c : c + CHUNK, :] + wide(col_ref[c : c + CHUNK, :], W) + u)
        e_ref[i, c : c + CHUNK, :] = e
        part = jnp.sum(e.reshape(CHUNK // 8, 8, W), axis=0)
        total = part if total is None else total + part
    sum_ref[:, row_slice(i, W)] = jnp.sum(total, axis=0, keepdims=True)
    copies = store(e_ref, stored_ref, sems, range(EARLY))
    for slab in range(EARLY):

        @pl.when(i == slab)
        def _(slab=slab):
            for copy in copies[slab * SPLIT : (slab + 1) * SPLIT]:
                copy.start()

    @pl.when(i == pl.num_programs(0) - 1)
    def _():
        for copy in copies:
            copy.wait()


def col_sums(e_ref, total_ref, fm_ref, held_ref, sum_ref, alpha_ref, share_ref, stored_ref, sems):
    i = pl.program_id(0)
    nf = fm_ref.shape[1]
    finish = during(store(e_ref, stored_ref, sems, range(EARLY, EARLY + 2)))

    @pl.when(i == 0)
    def _():
        alpha = fm_ref[...] / total_ref[:, :nf]
        alpha_ref[...] = alpha
        share_ref[...] = alpha / wide(total_ref[:, nf : nf + 128], nf)

    step = 64
    found = []
    for r in range(0, TOK, step):
        rows = pl.ds(pl.multiple_of(i * TOK + r, step), step)
        total = None
        for c in range(e_ref.shape[0]):
            p = e_ref[c, rows, :] * alpha_ref[:, c * W : (c + 1) * W]
            for w in range(0, W, 128):
                part = p[:, w : w + 128]
                total = part if total is None else total + part
        found.append(total)
    sum_ref[...] = jnp.sum(jnp.concatenate(found).T, axis=0, keepdims=True)
    finish()


def token_parts(first, slabs, e_ref, alpha_ref, f_ref, *refs):
    out_ref, stored_ref, sems = refs[-3:]
    finish = during(store(e_ref, stored_ref, sems, slabs))
    rows = row_slice(first + pl.program_id(0), TOK)
    acc = None
    for c in range(e_ref.shape[0]):
        p = (e_ref[c, rows, :] * alpha_ref[:, c * W : (c + 1) * W]).astype(BF16)
        part = jnp.dot(p, f_ref[c * W : (c + 1) * W, :], preferred_element_type=F32)
        acc = part if acc is None else acc + part
    out_ref[...] = acc.astype(BF16)
    finish()


def frame_parts(
    base_ref, e_ref, total_ref, tm_ref, share_ref, turned_ref, sum_ref, theirs_ref, mine_ref,
    col_ref, held_ref, tt_ref, sems, tt_sem,
):
    i = pl.program_id(0)
    slabs = pl.num_programs(0)

    def fetch(k):
        slot = lax.rem(k, HELD)
        return pltpu.make_async_copy(e_ref.at[lax.rem(base_ref[0] + k, slabs)], held_ref.at[slot], sems.at[slot])

    @pl.when(i == 0)
    def _():
        fetch(0).start()
        copy = pltpu.make_async_copy(turned_ref, tt_ref, tt_sem)
        copy.start()
        for k in range(1, HELD - 1):
            fetch(k).start()
        column(tm_ref[...] / total_ref[...], col_ref)
        copy.wait()

    @pl.when(i + HELD - 1 < slabs)
    def _():
        fetch(i + HELD - 1).start()

    fetch(i).wait()
    share = share_ref[:, row_slice(lax.rem(base_ref[0] + i, slabs), W)]
    p = held_ref[lax.rem(i, HELD)] * wide(col_ref[...], W) * share
    sum_ref[...] = jnp.sum(p, axis=0, keepdims=True)
    block = jnp.dot(tt_ref[...], p.astype(BF16), preferred_element_type=F32).T.astype(BF16)

    @pl.when(i < slabs // 2)
    def _():
        theirs_ref[...] = block

    @pl.when(i >= slabs // 2)
    def _():
        mine_ref[...] = block


def sum_pieces(*refs):
    total_ref, out_ref, col_ref = refs[-3:]
    column(total_ref[...], col_ref)
    rows, d = refs[0].shape[1:]
    for k, pieces_ref in enumerate(refs[:-3]):
        acc = pieces_ref[0].astype(F32)
        for n in range(1, pieces_ref.shape[0]):
            acc = acc + pieces_ref[n].astype(F32)
        some = slice(k * rows, (k + 1) * rows)
        out_ref[some, :] = (acc / wide(col_ref[some, :], d)).astype(BF16)


def deal_pieces(plane_ref, mine_ref, other_ref, out_ref, sems):
    rows = mine_ref.shape[0]
    copies = [
        pltpu.make_async_copy(ref, out_ref.at[k, row_slice(which, rows), :], sems.at[k, n])
        for k in range(out_ref.shape[0])
        for n, (ref, which) in enumerate(((mine_ref, plane_ref[0]), (other_ref, 1 - plane_ref[0])))
    ]
    for copy in copies:
        copy.start()
    for copy in copies:
        copy.wait()


def place_tokens(pieces_ref, out_ref, held_ref, sems, out_sems):
    count, rows = pieces_ref.shape[0], pieces_ref.shape[1]
    ins = [pltpu.make_async_copy(pieces_ref.at[k], held_ref.at[k], sems.at[k]) for k in range(count)]
    half, piece = out_ref.shape[0] // 2, rows // 2
    outs = [
        pltpu.make_async_copy(
            held_ref.at[k, pl.ds(n * piece, piece), :],
            out_ref.at[pl.ds(n * half + k * piece, piece), :],
            out_sems.at[k, n],
        )
        for k in range(count)
        for n in range(2)
    ]
    for copy in ins:
        copy.start()
    for k in range(count):
        ins[k].wait()
        outs[2 * k].start()
        outs[2 * k + 1].start()
    for copy in outs:
        copy.wait()


def finish_frames(core_ref, mine_ref, other_ref, total_ref, out_ref, map_ref, col_ref, sem):
    column(total_ref[...], col_ref)
    rows, d = mine_ref.shape
    for r in range(0, rows, 128):
        some = slice(r, r + 128)
        done = (mine_ref[some, :].astype(F32) + other_ref[some, :].astype(F32)) / wide(col_ref[some, :], d)
        out_ref[some, :] = done.astype(BF16)
    copy = pltpu.make_async_copy(out_ref, map_ref.at[row_slice(core_ref[0], rows), :], sem)
    copy.start()
    copy.wait()


def whole(*shape):
    return pl.BlockSpec(shape, lambda i: (0,) * len(shape))


def rows(size, width):
    return pl.BlockSpec((size, width), lambda i: (i, 0))


def lanes(size):
    return pl.BlockSpec((1, size), lambda i: (0, i))


def f32(*shape):
    return jax.ShapeDtypeStruct(shape, F32)


def call(body, steps, in_specs, out_specs, out_shape, scratch=(), **kwargs):
    return pl.pallas_call(
        body,
        grid=(steps,),
        in_specs=in_specs,
        out_specs=out_specs,
        out_shape=out_shape,
        scratch_shapes=scratch,
        compiler_params=pltpu.CompilerParams(vmem_limit_bytes=VMEM_BYTES),
        **kwargs,
    )


def shards(frames, tokens, frame_mass, token_mass):
    nf, d = frames.shape
    nt = tokens.shape[0]
    n_ctx = lax.axis_size("ctx")
    scale = math.log2(math.e) / math.sqrt(d)
    fm, tm = frame_mass.reshape(1, nf), token_mass.reshape(1, nt)
    slabs, steps = nf // W, nt // TOK
    kept = pltpu.VMEM((slabs, nt, W), F32)
    ctx, core = lax.axis_index("ctx"), lax.axis_index("tok") % 2
    hbm = pl.BlockSpec(memory_space=pltpu.HBM)

    lse, s = call(
        functools.partial(first_rows, scale), slabs // PAIR,
        [pl.BlockSpec((nt // SPLIT, d), lambda i, k=k: (k, 0)) for k in range(SPLIT)] + [rows(PAIR * W, d)],
        [lanes(PAIR * W), VMEM], [f32(1, nf), kept], name="first_rows",
    )(*[pltpu.with_memory_space_constraint(tokens, pltpu.HBM)] * SPLIT, pltpu.with_memory_space_constraint(frames, pltpu.HBM))
    with jax.named_scope("rows_one"):
        lse = merge_lse([lse, swap_tok(lse, 1)])
        lse = merge_lse([lse, swap_tok(lse, 2)])
    lse, u, frame_total = call(
        first_cols, steps, [VMEM, whole(1, nf), whole(1, nf)], [lanes(TOK), whole(1, nf), whole(1, 128)],
        [f32(1, nt), f32(1, nf), f32(1, 128)], name="first_cols",
    )(s, lse, fm)
    with jax.named_scope("cols_one"):
        lse = jnp.concatenate([lse, frame_total], axis=1)
        parts = lax.all_to_all(jnp.broadcast_to(lse[None], (n_ctx, 1, nt + 128)), "ctx", 0, 0)[:, 0]
        highest = jnp.max(parts[:, :nt], axis=0, keepdims=True)
        lse = highest + log2(jnp.sum(jnp.exp2(parts[:, :nt] - highest), axis=0, keepdims=True))
        frame_total = jnp.sum(parts[:, nt])
    part, e, stored = call(
        second_rows, slabs, [VMEM, whole(1, nt), whole(1, nt), whole(1, nf)], [whole(1, nf + EXTRA), VMEM, hbm],
        [f32(1, nf + EXTRA), kept, pltpu.HBM((slabs, nt, W), F32)],
        [pltpu.VMEM((nt, 128), F32), pltpu.SemaphoreType.DMA((EARLY, SPLIT))],
        input_output_aliases={0: 1}, name="second_rows",
    )(s, lse, tm, u)
    with jax.named_scope("rows_two"):
        part = part + swap_tok(part, 1)
        tokens_later, part = lax.optimization_barrier((tokens, part))
        turned = call(
            turn, 4, [rows(nt // 4, d)], pl.BlockSpec((d, nt // 4), lambda i: (0, i)),
            pltpu.HBM((d, nt), BF16), name="turn",
        )(tokens_later)
        part = part + swap_tok(part, 2)
        part, turned = lax.optimization_barrier((part, turned))
    part, alpha, share, stored = call(
        col_sums, steps, [VMEM, whole(1, nf + EXTRA), whole(1, nf), hbm],
        [lanes(TOK), whole(1, nf), whole(1, nf), hbm],
        [f32(1, nt), f32(1, nf), f32(1, nf), pltpu.HBM((slabs, nt, W), F32)],
        [pltpu.SemaphoreType.DMA((2, SPLIT))], input_output_aliases={3: 3}, name="col_sums",
    )(e, part, fm, stored)

    def some_token_parts(first, count, late, stored, held):
        return call(
            functools.partial(token_parts, first, late), count, [VMEM, whole(1, nf), VMEM, hbm] + [hbm] * len(held),
            [pl.BlockSpec((TOK, d), lambda i: (first + i, 0)), hbm],
            [pltpu.HBM((nt, d), BF16), pltpu.HBM((slabs, nt, W), F32)], [pltpu.SemaphoreType.DMA((1, SPLIT))],
            input_output_aliases={3: 1} | {4 + k: 0 for k in range(len(held))}, name="token_parts",
        )(e, alpha, frames, stored, *held)

    with jax.named_scope("cols_two"):
        held, first = [], 0
        late = list(range(EARLY + 2, slabs))
        col_total = part
        for stride, size, later, count in STAGES:
            which = [late.pop()] if late and count > 1 else []
            token_part, stored = some_token_parts(first, count, which, stored, held)
            first += count
            col_total = col_total + meet(col_total, stride, size, later)
            col_total, token_part = lax.optimization_barrier((col_total, token_part))
            held = [token_part]
    with jax.named_scope("token_scatter"):
        plane, own = 16, nt // n_ctx
        planes = [list(range(z, z + plane)) for z in range(0, n_ctx, plane)]
        pieces = lax.all_to_all(token_part.reshape(n_ctx, own, d), "ctx", 0, 0)

    e = pltpu.with_memory_space_constraint(stored, pltpu.HBM)
    half = slabs // 2
    base = ((1 - core) * half).reshape(1).astype(jnp.int32)
    with jax.named_scope("frame_rows"):
        sums, theirs, mine = pl.pallas_call(
            frame_parts,
            grid=(slabs,),
            in_specs=[SMEM, hbm, whole(1, nt), whole(1, nt), whole(1, nf), hbm],
            out_specs=[
                lanes(W),
                pl.BlockSpec((W, d), lambda i: (jnp.minimum(i, half - 1), 0)),
                pl.BlockSpec((W, d), lambda i: (jnp.maximum(i - half, 0), 0)),
            ],
            out_shape=[f32(1, nf)] + [jax.ShapeDtypeStruct((nf // 2, d), BF16)] * 2,
            scratch_shapes=[
                pltpu.VMEM((nt, 128), F32),
                pltpu.VMEM((HELD, nt, W), F32),
                pltpu.VMEM((d, nt), BF16),
                pltpu.SemaphoreType.DMA((HELD,)),
                pltpu.SemaphoreType.DMA,
            ],
            compiler_params=pltpu.CompilerParams(vmem_limit_bytes=VMEM_BYTES),
            name="frame_parts",
        )(base, e, col_total, tm, share, pltpu.with_memory_space_constraint(turned, pltpu.HBM))
        my_sum = sums[:, nf // 2 :] + swap_tok(sums[:, : nf // 2], 1)
        other_sum = swap_tok(my_sum, 2)
        mine = (mine.astype(F32) + swap_tok(theirs, 1).astype(F32)).astype(BF16)
    with jax.named_scope("token_sums"):
        pieces, mine = lax.optimization_barrier((pieces, mine))
        col_mine = lax.dynamic_slice_in_dim(col_total, ctx * own, own, axis=1)
        deal = own // SPLIT
        piece = call(
            sum_pieces, 1,
            [pl.BlockSpec((n_ctx, deal, d), lambda i, k=k: (0, k, 0)) for k in range(SPLIT)] + [whole(1, 128)],
            rows(own, d), jax.ShapeDtypeStruct((own, d), BF16), [pltpu.VMEM((128, 128), F32)], name="sum_pieces",
        )(*[pieces] * SPLIT, jnp.pad(col_mine, ((0, 0), (0, 128 - own)), constant_values=1.0))
        other_piece = meet(piece, 16, 2, 0)
        mine, other_piece = lax.optimization_barrier((mine, other_piece))
        other = swap_tok(mine, 2)
    with jax.named_scope("token_gather"):
        pieces = pl.pallas_call(
            deal_pieces, in_specs=[SMEM] + [VMEM] * 2, out_specs=hbm, out_shape=pltpu.HBM((plane, 2 * own, d), BF16),
            scratch_shapes=[pltpu.SemaphoreType.DMA((plane, 2))],
            compiler_params=pltpu.CompilerParams(vmem_limit_bytes=VMEM_BYTES), name="deal_pieces",
        )((ctx // plane).reshape(1).astype(jnp.int32), piece, other_piece)
        pieces = lax.all_to_all(pieces, "ctx", 0, 0, axis_index_groups=planes)
    with jax.named_scope("frame_sums"):
        my_sum = my_sum + other_sum
        their_sum = swap_tok(my_sum, 1)
        low = jnp.where(core == 0, my_sum, their_sum)
        high = jnp.where(core == 0, their_sum, my_sum)
        row_sum = jnp.concatenate([low, high], axis=1)[0]
        mass_ratio = row_sum / (frame_mass / frame_total)
    with jax.named_scope("frame_out"):
        which = core.reshape(1).astype(jnp.int32)
        mine, frame_map = pl.pallas_call(
            finish_frames, in_specs=[SMEM] + [VMEM] * 3, out_specs=[VMEM, hbm],
            out_shape=[jax.ShapeDtypeStruct((nf // 2, d), BF16), pltpu.HBM((nf, d), BF16)],
            scratch_shapes=[pltpu.VMEM((nf // 2, 128), F32), pltpu.SemaphoreType.DMA],
            compiler_params=pltpu.CompilerParams(vmem_limit_bytes=VMEM_BYTES), name="finish_frames",
        )(which, mine, other, my_sum)
        frame_map = lax.dynamic_update_slice_in_dim(frame_map, swap_tok(mine, 1), (1 - core) * (nf // 2), 0)
        pieces, frame_map = lax.optimization_barrier((pieces, frame_map))
        token_map = pl.pallas_call(
            place_tokens, in_specs=[hbm], out_specs=hbm, out_shape=pltpu.HBM((nt, d), BF16),
            scratch_shapes=[
                pltpu.VMEM((plane, 2 * own, d), BF16),
                pltpu.SemaphoreType.DMA((plane,)),
                pltpu.SemaphoreType.DMA((plane, 2)),
            ],
            compiler_params=pltpu.CompilerParams(vmem_limit_bytes=VMEM_BYTES), name="place_tokens",
        )(pltpu.with_memory_space_constraint(pieces, pltpu.HBM))
    return frame_map, token_map, mass_ratio


def solution(mesh):
    return jax.shard_map(
        shards,
        mesh=mesh,
        in_specs=(P("ctx", None), P("tok", None), P("ctx"), P("tok")),
        out_specs=(P("ctx", None), P("tok", None), P("ctx")),
        check_vma=False,
    )
```

```python
import functools
import math

import jax
import jax.numpy as jnp
from jax import lax
from jax.experimental import pallas as pl
from jax.experimental.pallas import tpu as pltpu
from jax.sharding import PartitionSpec as P

F32, BF16 = jnp.float32, jnp.bfloat16
W = 256
TOK = 256
CHUNK = 128
SPLIT = 4
STAGES = ((16, 2, 0, 2), (1, 4, 0, 1), (1, 4, 1, 2), (4, 4, 0, 1), (4, 4, 1, 2))
EARLY = 4
HELD = 4
PAIR = 1
EXTRA = 256
VMEM_BYTES = 20 * 1024 * 1024
VMEM = pl.BlockSpec(memory_space=pltpu.VMEM)
SMEM = pl.BlockSpec(memory_space=pltpu.SMEM)
ANY = pl.BlockSpec(memory_space=pl.ANY)


def swap_tok(value, bit):
    return lax.ppermute(value, "tok", [(i, i ^ bit) for i in range(lax.axis_size("tok"))])


def meet(value, stride, size, later):
    pairs = []
    for i in range(lax.axis_size("ctx")):
        c = i // stride % size
        other = c + 1 if c % 2 == later else c - 1
        pairs.append((i, i + (other % size - c) * stride))
    return lax.ppermute(value, "ctx", pairs)


def log2(x):
    return jnp.log(x) * (1.0 / math.log(2.0))


def column(row, out_ref):
    for start in range(0, row.shape[1], 128):
        block = jnp.broadcast_to(row[:, start : start + 128], (128, 128))
        out_ref[start : start + 128, :] = block.T


def wide(col, width):
    return jnp.concatenate([col] * (width // 128), axis=1)


def merge_lse(parts):
    highest = functools.reduce(jnp.maximum, parts)
    return highest + log2(sum(jnp.exp2(part - highest) for part in parts))


def row_slice(i, size):
    return pl.ds(pl.multiple_of(i * size, size), size)


def turn(in_ref, out_ref):
    out_ref[...] = in_ref[...].T


def first_rows(scale, *refs):
    t_refs, (f_ref, lse_ref, s_ref) = refs[:SPLIT], refs[SPLIT:]
    i = pl.program_id(0)
    tokens = jnp.concatenate([t_ref[...] for t_ref in t_refs])
    product = lax.dot_general(tokens, f_ref[...], (((1,), (1,)), ((), ())), preferred_element_type=F32) * scale
    count = f_ref.shape[0] // W
    for n in range(count):
        s_ref[i * count + n] = product[:, n * W : (n + 1) * W]
    for n in range(count):
        highest = total = None
        for c in range(0, tokens.shape[0], CHUNK):
            s = s_ref[i * count + n, c : c + CHUNK, :].reshape(CHUNK // 8, 8, W)
            top = jnp.max(s, axis=0)
            if highest is None:
                highest = top
                total = jnp.sum(jnp.exp2(s - highest[None]), axis=0)
            else:
                top = jnp.maximum(highest, top)
                total = total * jnp.exp2(highest - top) + jnp.sum(jnp.exp2(s - top[None]), axis=0)
                highest = top
        top = jnp.max(highest, axis=0, keepdims=True)
        lse = top + log2(jnp.sum(total * jnp.exp2(highest - top), axis=0, keepdims=True))
        lse_ref[:, n * W : (n + 1) * W] = lse


def first_cols(s_ref, all_ref, fm_ref, lse_ref, u_ref, mass_ref):
    i = pl.program_id(0)

    @pl.when(i == 0)
    def _():
        u_ref[...] = log2(fm_ref[...]) - all_ref[...]
        mass_ref[...] = jnp.broadcast_to(jnp.sum(fm_ref[...]).reshape(1, 1), (1, 128))

    step = 16
    found = []
    for r in range(0, TOK, step):
        rows = pl.ds(pl.multiple_of(i * TOK + r, step), step)
        tiles = [
            s_ref[c, rows, w : w + 128] + u_ref[:, c * W + w : c * W + w + 128]
            for c in range(s_ref.shape[0])
            for w in range(0, W, 128)
        ]
        highest = functools.reduce(jnp.maximum, tiles)
        total = sum(jnp.exp2(tile - highest) for tile in tiles)
        top = jnp.max(highest, axis=1, keepdims=True)
        lse = top + log2(jnp.sum(total * jnp.exp2(highest - top), axis=1, keepdims=True))
        found.append(jnp.broadcast_to(lse, (step, 128)))
    lse_ref[...] = jnp.concatenate(found).T[0:1]


def store(e_ref, stored_ref, sems, slabs):
    size = e_ref.shape[1] // SPLIT
    return [
        pltpu.make_async_copy(
            e_ref.at[slab, pl.ds(k * size, size), :], stored_ref.at[slab, pl.ds(k * size, size), :], sems.at[n, k]
        )
        for n, slab in enumerate(slabs)
        for k in range(SPLIT)
    ]


def during(copies):
    @pl.when(pl.program_id(0) == 0)
    def _():
        for copy in copies:
            copy.start()

    def finish():
        @pl.when(pl.program_id(0) == pl.num_programs(0) - 1)
        def _():
            for copy in copies:
                copy.wait()

    return finish


def second_rows(s_ref, parts_ref, tm_ref, u_ref, sum_ref, mass_ref, e_ref, stored_ref, col_ref, sems):
    i = pl.program_id(0)
    nt = s_ref.shape[1]
    nf = u_ref.shape[1]

    @pl.when(i == 0)
    def _():
        parts = parts_ref[:, :nt]
        highest = jnp.max(parts, axis=0, keepdims=True)
        merged = highest + log2(jnp.sum(jnp.exp2(parts - highest), axis=0, keepdims=True))
        column(log2(tm_ref[...]) - merged, col_ref)
        mass_ref[...] = jnp.sum(parts_ref[:, nt:], axis=0, keepdims=True)
        sum_ref[:, nf:] = jnp.broadcast_to(jnp.sum(tm_ref[...]).reshape(1, 1), (1, EXTRA))

    u = u_ref[:, row_slice(i, W)]
    total = None
    for c in range(0, nt, CHUNK):
        e = jnp.exp2(s_ref[i, c : c + CHUNK, :] + wide(col_ref[c : c + CHUNK, :], W) + u)
        e_ref[i, c : c + CHUNK, :] = e
        part = jnp.sum(e.reshape(CHUNK // 8, 8, W), axis=0)
        total = part if total is None else total + part
    sum_ref[:, row_slice(i, W)] = jnp.sum(total, axis=0, keepdims=True)
    copies = store(e_ref, stored_ref, sems, range(EARLY))
    for slab in range(EARLY):

        @pl.when(i == slab)
        def _(slab=slab):
            for copy in copies[slab * SPLIT : (slab + 1) * SPLIT]:
                copy.start()

    @pl.when(i == pl.num_programs(0) - 1)
    def _():
        for copy in copies:
            copy.wait()


def col_sums(e_ref, total_ref, fm_ref, held_ref, sum_ref, alpha_ref, share_ref, stored_ref, sems):
    i = pl.program_id(0)
    nf = fm_ref.shape[1]
    finish = during(store(e_ref, stored_ref, sems, range(EARLY, EARLY + 2)))

    @pl.when(i == 0)
    def _():
        alpha = fm_ref[...] / total_ref[:, :nf]
        alpha_ref[...] = alpha
        share_ref[...] = alpha / wide(total_ref[:, nf : nf + 128], nf)

    step = 64
    found = []
    for r in range(0, TOK, step):
        rows = pl.ds(pl.multiple_of(i * TOK + r, step), step)
        total = None
        for c in range(e_ref.shape[0]):
            p = e_ref[c, rows, :] * alpha_ref[:, c * W : (c + 1) * W]
            for w in range(0, W, 128):
                part = p[:, w : w + 128]
                total = part if total is None else total + part
        found.append(total)
    sum_ref[...] = jnp.sum(jnp.concatenate(found).T, axis=0, keepdims=True)
    finish()


def token_parts(first, slabs, e_ref, alpha_ref, f_ref, *refs):
    out_ref, stored_ref, sems = refs[-3:]
    finish = during(store(e_ref, stored_ref, sems, slabs))
    rows = row_slice(first + pl.program_id(0), TOK)
    acc = None
    for c in range(e_ref.shape[0]):
        p = (e_ref[c, rows, :] * alpha_ref[:, c * W : (c + 1) * W]).astype(BF16)
        part = jnp.dot(p, f_ref[c * W : (c + 1) * W, :], preferred_element_type=F32)
        acc = part if acc is None else acc + part
    out_ref[...] = acc.astype(BF16)
    finish()


def frame_parts(
    base_ref, e_ref, total_ref, tm_ref, share_ref, turned_ref, sum_ref, theirs_ref, mine_ref,
    col_ref, held_ref, tt_ref, sems, tt_sem,
):
    i = pl.program_id(0)
    slabs = pl.num_programs(0)

    def fetch(k):
        slot = lax.rem(k, HELD)
        return pltpu.make_async_copy(e_ref.at[lax.rem(base_ref[0] + k, slabs)], held_ref.at[slot], sems.at[slot])

    @pl.when(i == 0)
    def _():
        fetch(0).start()
        copy = pltpu.make_async_copy(turned_ref, tt_ref, tt_sem)
        copy.start()
        for k in range(1, HELD - 1):
            fetch(k).start()
        column(tm_ref[...] / total_ref[...], col_ref)
        copy.wait()

    @pl.when(i + HELD - 1 < slabs)
    def _():
        fetch(i + HELD - 1).start()

    fetch(i).wait()
    share = share_ref[:, row_slice(lax.rem(base_ref[0] + i, slabs), W)]
    p = held_ref[lax.rem(i, HELD)] * wide(col_ref[...], W) * share
    sum_ref[...] = jnp.sum(p, axis=0, keepdims=True)
    block = jnp.dot(tt_ref[...], p.astype(BF16), preferred_element_type=F32).T.astype(BF16)

    @pl.when(i < slabs // 2)
    def _():
        theirs_ref[...] = block

    @pl.when(i >= slabs // 2)
    def _():
        mine_ref[...] = block


def sum_pieces(*refs):
    total_ref, out_ref, col_ref = refs[-3:]
    column(total_ref[...], col_ref)
    rows, d = refs[0].shape[1:]
    for k, pieces_ref in enumerate(refs[:-3]):
        acc = pieces_ref[0].astype(F32)
        for n in range(1, pieces_ref.shape[0]):
            acc = acc + pieces_ref[n].astype(F32)
        some = slice(k * rows, (k + 1) * rows)
        out_ref[some, :] = (acc / wide(col_ref[some, :], d)).astype(BF16)


def deal_pieces(plane_ref, mine_ref, other_ref, out_ref, sems):
    rows = mine_ref.shape[0]
    copies = [
        pltpu.make_async_copy(ref, out_ref.at[k, row_slice(which, rows), :], sems.at[k, n])
        for k in range(out_ref.shape[0])
        for n, (ref, which) in enumerate(((mine_ref, plane_ref[0]), (other_ref, 1 - plane_ref[0])))
    ]
    for copy in copies:
        copy.start()
    for copy in copies:
        copy.wait()


def place_tokens(pieces_ref, out_ref, held_ref, sems, out_sems):
    count, rows = pieces_ref.shape[0], pieces_ref.shape[1]
    ins = [pltpu.make_async_copy(pieces_ref.at[k], held_ref.at[k], sems.at[k]) for k in range(count)]
    half, piece = out_ref.shape[0] // 2, rows // 2
    outs = [
        pltpu.make_async_copy(
            held_ref.at[k, pl.ds(n * piece, piece), :],
            out_ref.at[pl.ds(n * half + k * piece, piece), :],
            out_sems.at[k, n],
        )
        for k in range(count)
        for n in range(2)
    ]
    for copy in ins:
        copy.start()
    for k in range(count):
        ins[k].wait()
        outs[2 * k].start()
        outs[2 * k + 1].start()
    for copy in outs:
        copy.wait()


def finish_frames(core_ref, mine_ref, other_ref, total_ref, out_ref, map_ref, col_ref, sem):
    column(total_ref[...], col_ref)
    rows, d = mine_ref.shape
    for r in range(0, rows, 128):
        some = slice(r, r + 128)
        done = (mine_ref[some, :].astype(F32) + other_ref[some, :].astype(F32)) / wide(col_ref[some, :], d)
        out_ref[some, :] = done.astype(BF16)
    copy = pltpu.make_async_copy(out_ref, map_ref.at[row_slice(core_ref[0], rows), :], sem)
    copy.start()
    copy.wait()


def whole(*shape):
    return pl.BlockSpec(shape, lambda i: (0,) * len(shape))


def rows(size, width):
    return pl.BlockSpec((size, width), lambda i: (i, 0))


def lanes(size):
    return pl.BlockSpec((1, size), lambda i: (0, i))


def f32(*shape):
    return jax.ShapeDtypeStruct(shape, F32)


def call(body, steps, in_specs, out_specs, out_shape, scratch=(), **kwargs):
    return pl.pallas_call(
        body,
        grid=(steps,),
        in_specs=in_specs,
        out_specs=out_specs,
        out_shape=out_shape,
        scratch_shapes=scratch,
        compiler_params=pltpu.CompilerParams(vmem_limit_bytes=VMEM_BYTES),
        **kwargs,
    )


def shards(frames, tokens, frame_mass, token_mass):
    nf, d = frames.shape
    nt = tokens.shape[0]
    n_ctx = lax.axis_size("ctx")
    scale = math.log2(math.e) / math.sqrt(d)
    fm, tm = frame_mass.reshape(1, nf), token_mass.reshape(1, nt)
    slabs, steps = nf // W, nt // TOK
    kept = pltpu.VMEM((slabs, nt, W), F32)
    ctx, core = lax.axis_index("ctx"), lax.axis_index("tok") % 2
    hbm = pl.BlockSpec(memory_space=pltpu.HBM)

    lse, s = call(
        functools.partial(first_rows, scale), slabs // PAIR,
        [pl.BlockSpec((nt // SPLIT, d), lambda i, k=k: (k, 0)) for k in range(SPLIT)] + [rows(PAIR * W, d)],
        [lanes(PAIR * W), VMEM], [f32(1, nf), kept], name="first_rows",
    )(*[pltpu.with_memory_space_constraint(tokens, pltpu.HBM)] * SPLIT, pltpu.with_memory_space_constraint(frames, pltpu.HBM))
    with jax.named_scope("rows_one"):
        lse = merge_lse([lse, swap_tok(lse, 1)])
        lse = merge_lse([lse, swap_tok(lse, 2)])
    lse, u, frame_total = call(
        first_cols, steps, [VMEM, whole(1, nf), whole(1, nf)], [lanes(TOK), whole(1, nf), whole(1, 128)],
        [f32(1, nt), f32(1, nf), f32(1, 128)], name="first_cols",
    )(s, lse, fm)
    with jax.named_scope("cols_one"):
        lse = jnp.concatenate([lse, frame_total], axis=1)
        parts = lax.all_to_all(jnp.broadcast_to(lse[None], (n_ctx, 1, nt + 128)), "ctx", 0, 0)[:, 0]
    part, frame_total, e, stored = call(
        second_rows, slabs, [VMEM, whole(n_ctx, nt + 128), whole(1, nt), whole(1, nf)],
        [whole(1, nf + EXTRA), whole(1, 128), VMEM, hbm], [f32(1, nf + EXTRA), f32(1, 128), kept, pltpu.HBM((slabs, nt, W), F32)],
        [pltpu.VMEM((nt, 128), F32), pltpu.SemaphoreType.DMA((EARLY, SPLIT))],
        input_output_aliases={0: 2}, name="second_rows",
    )(s, parts, tm, u)
    with jax.named_scope("rows_two"):
        part = part + swap_tok(part, 1)
        tokens_later, part = lax.optimization_barrier((tokens, part))
        turned = call(
            turn, 4, [rows(nt // 4, d)], pl.BlockSpec((d, nt // 4), lambda i: (0, i)),
            pltpu.HBM((d, nt), BF16), name="turn",
        )(tokens_later)
        part = part + swap_tok(part, 2)
        part, turned = lax.optimization_barrier((part, turned))
    part, alpha, share, stored = call(
        col_sums, steps, [VMEM, whole(1, nf + EXTRA), whole(1, nf), hbm],
        [lanes(TOK), whole(1, nf), whole(1, nf), hbm],
        [f32(1, nt), f32(1, nf), f32(1, nf), pltpu.HBM((slabs, nt, W), F32)],
        [pltpu.SemaphoreType.DMA((2, SPLIT))], input_output_aliases={3: 3}, name="col_sums",
    )(e, part, fm, stored)

    def some_token_parts(first, count, late, stored, held):
        return call(
            functools.partial(token_parts, first, late), count, [VMEM, whole(1, nf), VMEM, hbm] + [hbm] * len(held),
            [pl.BlockSpec((TOK, d), lambda i: (first + i, 0)), hbm],
            [pltpu.HBM((nt, d), BF16), pltpu.HBM((slabs, nt, W), F32)], [pltpu.SemaphoreType.DMA((1, SPLIT))],
            input_output_aliases={3: 1} | {4 + k: 0 for k in range(len(held))}, name="token_parts",
        )(e, alpha, frames, stored, *held)

    with jax.named_scope("cols_two"):
        held, first = [], 0
        late = list(range(EARLY + 2, slabs))
        col_total = part
        for stride, size, later, count in STAGES:
            which = [late.pop()] if late and count > 1 else []
            token_part, stored = some_token_parts(first, count, which, stored, held)
            first += count
            col_total = col_total + meet(col_total, stride, size, later)
            col_total, token_part = lax.optimization_barrier((col_total, token_part))
            held = [token_part]
    with jax.named_scope("token_scatter"):
        plane, own = 16, nt // n_ctx
        planes = [list(range(z, z + plane)) for z in range(0, n_ctx, plane)]
        pieces = lax.all_to_all(token_part.reshape(n_ctx, own, d), "ctx", 0, 0)

    e = pltpu.with_memory_space_constraint(stored, pltpu.HBM)
    half = slabs // 2
    base = ((1 - core) * half).reshape(1).astype(jnp.int32)
    with jax.named_scope("frame_rows"):
        sums, theirs, mine = pl.pallas_call(
            frame_parts,
            grid=(slabs,),
            in_specs=[SMEM, hbm, whole(1, nt), whole(1, nt), whole(1, nf), hbm],
            out_specs=[
                lanes(W),
                pl.BlockSpec((W, d), lambda i: (jnp.minimum(i, half - 1), 0)),
                pl.BlockSpec((W, d), lambda i: (jnp.maximum(i - half, 0), 0)),
            ],
            out_shape=[f32(1, nf)] + [jax.ShapeDtypeStruct((nf // 2, d), BF16)] * 2,
            scratch_shapes=[
                pltpu.VMEM((nt, 128), F32),
                pltpu.VMEM((HELD, nt, W), F32),
                pltpu.VMEM((d, nt), BF16),
                pltpu.SemaphoreType.DMA((HELD,)),
                pltpu.SemaphoreType.DMA,
            ],
            compiler_params=pltpu.CompilerParams(vmem_limit_bytes=VMEM_BYTES),
            name="frame_parts",
        )(base, e, col_total, tm, share, pltpu.with_memory_space_constraint(turned, pltpu.HBM))
        my_sum = sums[:, nf // 2 :] + swap_tok(sums[:, : nf // 2], 1)
        other_sum = swap_tok(my_sum, 2)
        mine = (mine.astype(F32) + swap_tok(theirs, 1).astype(F32)).astype(BF16)
    with jax.named_scope("token_sums"):
        pieces, mine = lax.optimization_barrier((pieces, mine))
        col_mine = lax.dynamic_slice_in_dim(col_total, ctx * own, own, axis=1)
        deal = own // SPLIT
        piece = call(
            sum_pieces, 1,
            [pl.BlockSpec((n_ctx, deal, d), lambda i, k=k: (0, k, 0)) for k in range(SPLIT)] + [whole(1, 128)],
            rows(own, d), jax.ShapeDtypeStruct((own, d), BF16), [pltpu.VMEM((128, 128), F32)], name="sum_pieces",
        )(*[pieces] * SPLIT, jnp.pad(col_mine, ((0, 0), (0, 128 - own)), constant_values=1.0))
        other_piece = meet(piece, 16, 2, 0)
        mine, other_piece = lax.optimization_barrier((mine, other_piece))
        other = swap_tok(mine, 2)
    with jax.named_scope("token_gather"):
        pieces = pl.pallas_call(
            deal_pieces, in_specs=[SMEM] + [VMEM] * 2, out_specs=hbm, out_shape=pltpu.HBM((plane, 2 * own, d), BF16),
            scratch_shapes=[pltpu.SemaphoreType.DMA((plane, 2))],
            compiler_params=pltpu.CompilerParams(vmem_limit_bytes=VMEM_BYTES), name="deal_pieces",
        )((ctx // plane).reshape(1).astype(jnp.int32), piece, other_piece)
        pieces = lax.all_to_all(pieces, "ctx", 0, 0, axis_index_groups=planes)
    with jax.named_scope("frame_sums"):
        my_sum = my_sum + other_sum
        their_sum = swap_tok(my_sum, 1)
        low = jnp.where(core == 0, my_sum, their_sum)
        high = jnp.where(core == 0, their_sum, my_sum)
        row_sum = jnp.concatenate([low, high], axis=1)[0]
        mass_ratio = row_sum / (frame_mass / frame_total[0, 0])
    with jax.named_scope("frame_out"):
        which = core.reshape(1).astype(jnp.int32)
        mine, frame_map = pl.pallas_call(
            finish_frames, in_specs=[SMEM] + [VMEM] * 3, out_specs=[VMEM, hbm],
            out_shape=[jax.ShapeDtypeStruct((nf // 2, d), BF16), pltpu.HBM((nf, d), BF16)],
            scratch_shapes=[pltpu.VMEM((nf // 2, 128), F32), pltpu.SemaphoreType.DMA],
            compiler_params=pltpu.CompilerParams(vmem_limit_bytes=VMEM_BYTES), name="finish_frames",
        )(which, mine, other, my_sum)
        frame_map = lax.dynamic_update_slice_in_dim(frame_map, swap_tok(mine, 1), (1 - core) * (nf // 2), 0)
        pieces, frame_map = lax.optimization_barrier((pieces, frame_map))
        token_map = pl.pallas_call(
            place_tokens, in_specs=[hbm], out_specs=hbm, out_shape=pltpu.HBM((nt, d), BF16),
            scratch_shapes=[
                pltpu.VMEM((plane, 2 * own, d), BF16),
                pltpu.SemaphoreType.DMA((plane,)),
                pltpu.SemaphoreType.DMA((plane, 2)),
            ],
            compiler_params=pltpu.CompilerParams(vmem_limit_bytes=VMEM_BYTES), name="place_tokens",
        )(pltpu.with_memory_space_constraint(pieces, pltpu.HBM))
    return frame_map, token_map, mass_ratio


def solution(mesh):
    return jax.shard_map(
        shards,
        mesh=mesh,
        in_specs=(P("ctx", None), P("tok", None), P("ctx"), P("tok")),
        out_specs=(P("ctx", None), P("tok", None), P("ctx")),
        check_vma=False,
    )
```

```python
import functools
import math

import jax
import jax.numpy as jnp
from jax import lax
from jax.experimental import pallas as pl
from jax.experimental.pallas import tpu as pltpu
from jax.sharding import PartitionSpec as P

F32, BF16 = jnp.float32, jnp.bfloat16
W = 256
TOK = 256
CHUNK = 128
SPLIT = 4
STAGES = ((16, 2, 0, 2), (1, 4, 0, 1), (1, 4, 1, 2), (4, 4, 0, 1), (4, 4, 1, 2))
EARLY = 4
HELD = 4
PAIR = 1
EXTRA = 256
VMEM_BYTES = 20 * 1024 * 1024
VMEM = pl.BlockSpec(memory_space=pltpu.VMEM)
SMEM = pl.BlockSpec(memory_space=pltpu.SMEM)
ANY = pl.BlockSpec(memory_space=pl.ANY)


def swap_tok(value, bit):
    return lax.ppermute(value, "tok", [(i, i ^ bit) for i in range(lax.axis_size("tok"))])


def meet(value, stride, size, later):
    pairs = []
    for i in range(lax.axis_size("ctx")):
        c = i // stride % size
        other = c + 1 if c % 2 == later else c - 1
        pairs.append((i, i + (other % size - c) * stride))
    return lax.ppermute(value, "ctx", pairs)


def log2(x):
    return jnp.log(x) * (1.0 / math.log(2.0))


def column(row, out_ref):
    for start in range(0, row.shape[1], 128):
        block = jnp.broadcast_to(row[:, start : start + 128], (128, 128))
        out_ref[start : start + 128, :] = block.T


def wide(col, width):
    return jnp.concatenate([col] * (width // 128), axis=1)


def merge_lse(parts):
    highest = functools.reduce(jnp.maximum, parts)
    return highest + log2(sum(jnp.exp2(part - highest) for part in parts))


def row_slice(i, size):
    return pl.ds(pl.multiple_of(i * size, size), size)


def turn(in_ref, out_ref):
    out_ref[...] = in_ref[...].T


def first_rows(scale, *refs):
    t_refs, (f_ref, lse_ref, s_ref) = refs[:SPLIT], refs[SPLIT:]
    i = pl.program_id(0)
    tokens = jnp.concatenate([t_ref[...] for t_ref in t_refs])
    product = lax.dot_general(tokens, f_ref[...], (((1,), (1,)), ((), ())), preferred_element_type=F32) * scale
    count = f_ref.shape[0] // W
    for n in range(count):
        s_ref[i * count + n] = product[:, n * W : (n + 1) * W]
    for n in range(count):
        highest = total = None
        for c in range(0, tokens.shape[0], CHUNK):
            s = s_ref[i * count + n, c : c + CHUNK, :].reshape(CHUNK // 8, 8, W)
            top = jnp.max(s, axis=0)
            if highest is None:
                highest = top
                total = jnp.sum(jnp.exp2(s - highest[None]), axis=0)
            else:
                top = jnp.maximum(highest, top)
                total = total * jnp.exp2(highest - top) + jnp.sum(jnp.exp2(s - top[None]), axis=0)
                highest = top
        top = jnp.max(highest, axis=0, keepdims=True)
        lse = top + log2(jnp.sum(total * jnp.exp2(highest - top), axis=0, keepdims=True))
        lse_ref[:, n * W : (n + 1) * W] = lse


def first_cols(s_ref, all_ref, fm_ref, lse_ref, u_ref):
    i = pl.program_id(0)
    nt, count = s_ref.shape[1], lse_ref.shape[0]

    @pl.when(i == 0)
    def _():
        u_ref[...] = log2(fm_ref[...]) - all_ref[...]
        lse_ref[:, :, nt:] = jnp.broadcast_to(jnp.sum(fm_ref[...]).reshape(1, 1, 1), (count, 1, 128))

    step = 16
    found = []
    for r in range(0, TOK, step):
        rows = pl.ds(pl.multiple_of(i * TOK + r, step), step)
        tiles = [
            s_ref[c, rows, w : w + 128] + u_ref[:, c * W + w : c * W + w + 128]
            for c in range(s_ref.shape[0])
            for w in range(0, W, 128)
        ]
        highest = functools.reduce(jnp.maximum, tiles)
        total = sum(jnp.exp2(tile - highest) for tile in tiles)
        top = jnp.max(highest, axis=1, keepdims=True)
        lse = top + log2(jnp.sum(total * jnp.exp2(highest - top), axis=1, keepdims=True))
        found.append(jnp.broadcast_to(lse, (step, 128)))
    row = jnp.concatenate(found).T[0:1]
    lse_ref[:, :, row_slice(i, TOK)] = jnp.broadcast_to(row[None], (count, 1, TOK))


def store(e_ref, stored_ref, sems, slabs):
    size = e_ref.shape[1] // SPLIT
    return [
        pltpu.make_async_copy(
            e_ref.at[slab, pl.ds(k * size, size), :], stored_ref.at[slab, pl.ds(k * size, size), :], sems.at[n, k]
        )
        for n, slab in enumerate(slabs)
        for k in range(SPLIT)
    ]


def during(copies):
    @pl.when(pl.program_id(0) == 0)
    def _():
        for copy in copies:
            copy.start()

    def finish():
        @pl.when(pl.program_id(0) == pl.num_programs(0) - 1)
        def _():
            for copy in copies:
                copy.wait()

    return finish


def second_rows(s_ref, parts_ref, tm_ref, u_ref, sum_ref, mass_ref, e_ref, stored_ref, col_ref, sems):
    i = pl.program_id(0)
    nt = s_ref.shape[1]
    nf = u_ref.shape[1]

    @pl.when(i == 0)
    def _():
        parts = parts_ref[:, :nt]
        highest = jnp.max(parts, axis=0, keepdims=True)
        merged = highest + log2(jnp.sum(jnp.exp2(parts - highest), axis=0, keepdims=True))
        column(log2(tm_ref[...]) - merged, col_ref)
        mass_ref[...] = jnp.sum(parts_ref[:, nt:], axis=0, keepdims=True)
        sum_ref[:, nf:] = jnp.broadcast_to(jnp.sum(tm_ref[...]).reshape(1, 1), (1, EXTRA))

    u = u_ref[:, row_slice(i, W)]
    total = None
    for c in range(0, nt, CHUNK):
        e = jnp.exp2(s_ref[i, c : c + CHUNK, :] + wide(col_ref[c : c + CHUNK, :], W) + u)
        e_ref[i, c : c + CHUNK, :] = e
        part = jnp.sum(e.reshape(CHUNK // 8, 8, W), axis=0)
        total = part if total is None else total + part
    sum_ref[:, row_slice(i, W)] = jnp.sum(total, axis=0, keepdims=True)
    copies = store(e_ref, stored_ref, sems, range(EARLY))
    for slab in range(EARLY):

        @pl.when(i == slab)
        def _(slab=slab):
            for copy in copies[slab * SPLIT : (slab + 1) * SPLIT]:
                copy.start()

    @pl.when(i == pl.num_programs(0) - 1)
    def _():
        for copy in copies:
            copy.wait()


def col_sums(e_ref, total_ref, fm_ref, held_ref, sum_ref, alpha_ref, share_ref, stored_ref, sems):
    i = pl.program_id(0)
    nf = fm_ref.shape[1]
    finish = during(store(e_ref, stored_ref, sems, range(EARLY, EARLY + 2)))

    @pl.when(i == 0)
    def _():
        alpha = fm_ref[...] / total_ref[:, :nf]
        alpha_ref[...] = alpha
        share_ref[...] = alpha / wide(total_ref[:, nf : nf + 128], nf)

    step = 64
    found = []
    for r in range(0, TOK, step):
        rows = pl.ds(pl.multiple_of(i * TOK + r, step), step)
        total = None
        for c in range(e_ref.shape[0]):
            p = e_ref[c, rows, :] * alpha_ref[:, c * W : (c + 1) * W]
            for w in range(0, W, 128):
                part = p[:, w : w + 128]
                total = part if total is None else total + part
        found.append(total)
    sum_ref[...] = jnp.sum(jnp.concatenate(found).T, axis=0, keepdims=True)
    finish()


def token_parts(first, slabs, e_ref, alpha_ref, f_ref, *refs):
    out_ref, stored_ref, sems = refs[-3:]
    finish = during(store(e_ref, stored_ref, sems, slabs))
    rows = row_slice(first + pl.program_id(0), TOK)
    acc = None
    for c in range(e_ref.shape[0]):
        p = (e_ref[c, rows, :] * alpha_ref[:, c * W : (c + 1) * W]).astype(BF16)
        part = jnp.dot(p, f_ref[c * W : (c + 1) * W, :], preferred_element_type=F32)
        acc = part if acc is None else acc + part
    out_ref[...] = acc.astype(BF16)
    finish()


def frame_parts(
    base_ref, e_ref, total_ref, tm_ref, share_ref, turned_ref, sum_ref, theirs_ref, mine_ref,
    col_ref, held_ref, tt_ref, sems, tt_sem,
):
    i = pl.program_id(0)
    slabs = pl.num_programs(0)

    def fetch(k):
        slot = lax.rem(k, HELD)
        return pltpu.make_async_copy(e_ref.at[lax.rem(base_ref[0] + k, slabs)], held_ref.at[slot], sems.at[slot])

    @pl.when(i == 0)
    def _():
        fetch(0).start()
        copy = pltpu.make_async_copy(turned_ref, tt_ref, tt_sem)
        copy.start()
        for k in range(1, HELD - 1):
            fetch(k).start()
        column(tm_ref[...] / total_ref[...], col_ref)
        copy.wait()

    @pl.when(i + HELD - 1 < slabs)
    def _():
        fetch(i + HELD - 1).start()

    fetch(i).wait()
    share = share_ref[:, row_slice(lax.rem(base_ref[0] + i, slabs), W)]
    p = held_ref[lax.rem(i, HELD)] * wide(col_ref[...], W) * share
    sum_ref[...] = jnp.sum(p, axis=0, keepdims=True)
    block = jnp.dot(tt_ref[...], p.astype(BF16), preferred_element_type=F32).T.astype(BF16)

    @pl.when(i < slabs // 2)
    def _():
        theirs_ref[...] = block

    @pl.when(i >= slabs // 2)
    def _():
        mine_ref[...] = block


def sum_pieces(*refs):
    total_ref, out_ref, col_ref = refs[-3:]
    column(total_ref[...], col_ref)
    rows, d = refs[0].shape[1:]
    for k, pieces_ref in enumerate(refs[:-3]):
        acc = pieces_ref[0].astype(F32)
        for n in range(1, pieces_ref.shape[0]):
            acc = acc + pieces_ref[n].astype(F32)
        some = slice(k * rows, (k + 1) * rows)
        out_ref[some, :] = (acc / wide(col_ref[some, :], d)).astype(BF16)


def deal_pieces(plane_ref, mine_ref, other_ref, out_ref, sems):
    rows = mine_ref.shape[0]
    copies = [
        pltpu.make_async_copy(ref, out_ref.at[k, row_slice(which, rows), :], sems.at[k, n])
        for k in range(out_ref.shape[0])
        for n, (ref, which) in enumerate(((mine_ref, plane_ref[0]), (other_ref, 1 - plane_ref[0])))
    ]
    for copy in copies:
        copy.start()
    for copy in copies:
        copy.wait()


def place_tokens(pieces_ref, out_ref, held_ref, sems, out_sems):
    count, rows = pieces_ref.shape[0], pieces_ref.shape[1]
    ins = [pltpu.make_async_copy(pieces_ref.at[k], held_ref.at[k], sems.at[k]) for k in range(count)]
    half, piece = out_ref.shape[0] // 2, rows // 2
    outs = [
        pltpu.make_async_copy(
            held_ref.at[k, pl.ds(n * piece, piece), :],
            out_ref.at[pl.ds(n * half + k * piece, piece), :],
            out_sems.at[k, n],
        )
        for k in range(count)
        for n in range(2)
    ]
    for copy in ins:
        copy.start()
    for k in range(count):
        ins[k].wait()
        outs[2 * k].start()
        outs[2 * k + 1].start()
    for copy in outs:
        copy.wait()


def finish_frames(core_ref, mine_ref, other_ref, total_ref, out_ref, map_ref, col_ref, sem):
    column(total_ref[...], col_ref)
    rows, d = mine_ref.shape
    for r in range(0, rows, 128):
        some = slice(r, r + 128)
        done = (mine_ref[some, :].astype(F32) + other_ref[some, :].astype(F32)) / wide(col_ref[some, :], d)
        out_ref[some, :] = done.astype(BF16)
    copy = pltpu.make_async_copy(out_ref, map_ref.at[row_slice(core_ref[0], rows), :], sem)
    copy.start()
    copy.wait()


def whole(*shape):
    return pl.BlockSpec(shape, lambda i: (0,) * len(shape))


def rows(size, width):
    return pl.BlockSpec((size, width), lambda i: (i, 0))


def lanes(size):
    return pl.BlockSpec((1, size), lambda i: (0, i))


def f32(*shape):
    return jax.ShapeDtypeStruct(shape, F32)


def call(body, steps, in_specs, out_specs, out_shape, scratch=(), **kwargs):
    return pl.pallas_call(
        body,
        grid=(steps,),
        in_specs=in_specs,
        out_specs=out_specs,
        out_shape=out_shape,
        scratch_shapes=scratch,
        compiler_params=pltpu.CompilerParams(vmem_limit_bytes=VMEM_BYTES),
        **kwargs,
    )


def shards(frames, tokens, frame_mass, token_mass):
    nf, d = frames.shape
    nt = tokens.shape[0]
    n_ctx = lax.axis_size("ctx")
    scale = math.log2(math.e) / math.sqrt(d)
    fm, tm = frame_mass.reshape(1, nf), token_mass.reshape(1, nt)
    slabs, steps = nf // W, nt // TOK
    kept = pltpu.VMEM((slabs, nt, W), F32)
    ctx, core = lax.axis_index("ctx"), lax.axis_index("tok") % 2
    hbm = pl.BlockSpec(memory_space=pltpu.HBM)

    lse, s = call(
        functools.partial(first_rows, scale), slabs // PAIR,
        [pl.BlockSpec((nt // SPLIT, d), lambda i, k=k: (k, 0)) for k in range(SPLIT)] + [rows(PAIR * W, d)],
        [lanes(PAIR * W), VMEM], [f32(1, nf), kept], name="first_rows",
    )(*[pltpu.with_memory_space_constraint(tokens, pltpu.HBM)] * SPLIT, pltpu.with_memory_space_constraint(frames, pltpu.HBM))
    with jax.named_scope("rows_one"):
        lse = merge_lse([lse, swap_tok(lse, 1)])
        lse = merge_lse([lse, swap_tok(lse, 2)])
    lse, u = call(
        first_cols, steps, [VMEM, whole(1, nf), whole(1, nf)], [whole(n_ctx, 1, nt + 128), whole(1, nf)],
        [f32(n_ctx, 1, nt + 128), f32(1, nf)], name="first_cols",
    )(s, lse, fm)
    with jax.named_scope("cols_one"):
        parts = lax.all_to_all(lse, "ctx", 0, 0)[:, 0]
    part, frame_total, e, stored = call(
        second_rows, slabs, [VMEM, whole(n_ctx, nt + 128), whole(1, nt), whole(1, nf)],
        [whole(1, nf + EXTRA), whole(1, 128), VMEM, hbm], [f32(1, nf + EXTRA), f32(1, 128), kept, pltpu.HBM((slabs, nt, W), F32)],
        [pltpu.VMEM((nt, 128), F32), pltpu.SemaphoreType.DMA((EARLY, SPLIT))],
        input_output_aliases={0: 2}, name="second_rows",
    )(s, parts, tm, u)
    with jax.named_scope("rows_two"):
        part = part + swap_tok(part, 1)
        tokens_later, part = lax.optimization_barrier((tokens, part))
        turned = call(
            turn, 4, [rows(nt // 4, d)], pl.BlockSpec((d, nt // 4), lambda i: (0, i)),
            pltpu.HBM((d, nt), BF16), name="turn",
        )(tokens_later)
        part = part + swap_tok(part, 2)
        part, turned = lax.optimization_barrier((part, turned))
    part, alpha, share, stored = call(
        col_sums, steps, [VMEM, whole(1, nf + EXTRA), whole(1, nf), hbm],
        [lanes(TOK), whole(1, nf), whole(1, nf), hbm],
        [f32(1, nt), f32(1, nf), f32(1, nf), pltpu.HBM((slabs, nt, W), F32)],
        [pltpu.SemaphoreType.DMA((2, SPLIT))], input_output_aliases={3: 3}, name="col_sums",
    )(e, part, fm, stored)

    def some_token_parts(first, count, late, stored, held):
        return call(
            functools.partial(token_parts, first, late), count, [VMEM, whole(1, nf), VMEM, hbm] + [hbm] * len(held),
            [pl.BlockSpec((TOK, d), lambda i: (first + i, 0)), hbm],
            [pltpu.HBM((nt, d), BF16), pltpu.HBM((slabs, nt, W), F32)], [pltpu.SemaphoreType.DMA((1, SPLIT))],
            input_output_aliases={3: 1} | {4 + k: 0 for k in range(len(held))}, name="token_parts",
        )(e, alpha, frames, stored, *held)

    with jax.named_scope("cols_two"):
        held, first = [], 0
        late = list(range(EARLY + 2, slabs))
        col_total = part
        for stride, size, later, count in STAGES:
            which = [late.pop()] if late and count > 1 else []
            token_part, stored = some_token_parts(first, count, which, stored, held)
            first += count
            col_total = col_total + meet(col_total, stride, size, later)
            col_total, token_part = lax.optimization_barrier((col_total, token_part))
            held = [token_part]
    with jax.named_scope("token_scatter"):
        plane, own = 16, nt // n_ctx
        planes = [list(range(z, z + plane)) for z in range(0, n_ctx, plane)]
        pieces = lax.all_to_all(token_part.reshape(n_ctx, own, d), "ctx", 0, 0)

    e = pltpu.with_memory_space_constraint(stored, pltpu.HBM)
    half = slabs // 2
    base = ((1 - core) * half).reshape(1).astype(jnp.int32)
    with jax.named_scope("frame_rows"):
        sums, theirs, mine = pl.pallas_call(
            frame_parts,
            grid=(slabs,),
            in_specs=[SMEM, hbm, whole(1, nt), whole(1, nt), whole(1, nf), hbm],
            out_specs=[
                lanes(W),
                pl.BlockSpec((W, d), lambda i: (jnp.minimum(i, half - 1), 0)),
                pl.BlockSpec((W, d), lambda i: (jnp.maximum(i - half, 0), 0)),
            ],
            out_shape=[f32(1, nf)] + [jax.ShapeDtypeStruct((nf // 2, d), BF16)] * 2,
            scratch_shapes=[
                pltpu.VMEM((nt, 128), F32),
                pltpu.VMEM((HELD, nt, W), F32),
                pltpu.VMEM((d, nt), BF16),
                pltpu.SemaphoreType.DMA((HELD,)),
                pltpu.SemaphoreType.DMA,
            ],
            compiler_params=pltpu.CompilerParams(vmem_limit_bytes=VMEM_BYTES),
            name="frame_parts",
        )(base, e, col_total, tm, share, pltpu.with_memory_space_constraint(turned, pltpu.HBM))
        my_sum = sums[:, nf // 2 :] + swap_tok(sums[:, : nf // 2], 1)
        other_sum = swap_tok(my_sum, 2)
        mine = (mine.astype(F32) + swap_tok(theirs, 1).astype(F32)).astype(BF16)
    with jax.named_scope("token_sums"):
        pieces, mine = lax.optimization_barrier((pieces, mine))
        col_mine = lax.dynamic_slice_in_dim(col_total, ctx * own, own, axis=1)
        deal = own // SPLIT
        piece = call(
            sum_pieces, 1,
            [pl.BlockSpec((n_ctx, deal, d), lambda i, k=k: (0, k, 0)) for k in range(SPLIT)] + [whole(1, 128)],
            rows(own, d), jax.ShapeDtypeStruct((own, d), BF16), [pltpu.VMEM((128, 128), F32)], name="sum_pieces",
        )(*[pieces] * SPLIT, jnp.pad(col_mine, ((0, 0), (0, 128 - own)), constant_values=1.0))
        other_piece = meet(piece, 16, 2, 0)
        mine, other_piece = lax.optimization_barrier((mine, other_piece))
        other = swap_tok(mine, 2)
    with jax.named_scope("token_gather"):
        pieces = pl.pallas_call(
            deal_pieces, in_specs=[SMEM] + [VMEM] * 2, out_specs=hbm, out_shape=pltpu.HBM((plane, 2 * own, d), BF16),
            scratch_shapes=[pltpu.SemaphoreType.DMA((plane, 2))],
            compiler_params=pltpu.CompilerParams(vmem_limit_bytes=VMEM_BYTES), name="deal_pieces",
        )((ctx // plane).reshape(1).astype(jnp.int32), piece, other_piece)
        pieces = lax.all_to_all(pieces, "ctx", 0, 0, axis_index_groups=planes)
    with jax.named_scope("frame_sums"):
        my_sum = my_sum + other_sum
        their_sum = swap_tok(my_sum, 1)
        low = jnp.where(core == 0, my_sum, their_sum)
        high = jnp.where(core == 0, their_sum, my_sum)
        row_sum = jnp.concatenate([low, high], axis=1)[0]
        mass_ratio = row_sum / (frame_mass / frame_total[0, 0])
    with jax.named_scope("frame_out"):
        which = core.reshape(1).astype(jnp.int32)
        mine, frame_map = pl.pallas_call(
            finish_frames, in_specs=[SMEM] + [VMEM] * 3, out_specs=[VMEM, hbm],
            out_shape=[jax.ShapeDtypeStruct((nf // 2, d), BF16), pltpu.HBM((nf, d), BF16)],
            scratch_shapes=[pltpu.VMEM((nf // 2, 128), F32), pltpu.SemaphoreType.DMA],
            compiler_params=pltpu.CompilerParams(vmem_limit_bytes=VMEM_BYTES), name="finish_frames",
        )(which, mine, other, my_sum)
        frame_map = lax.dynamic_update_slice_in_dim(frame_map, swap_tok(mine, 1), (1 - core) * (nf // 2), 0)
        pieces, frame_map = lax.optimization_barrier((pieces, frame_map))
        token_map = pl.pallas_call(
            place_tokens, in_specs=[hbm], out_specs=hbm, out_shape=pltpu.HBM((nt, d), BF16),
            scratch_shapes=[
                pltpu.VMEM((plane, 2 * own, d), BF16),
                pltpu.SemaphoreType.DMA((plane,)),
                pltpu.SemaphoreType.DMA((plane, 2)),
            ],
            compiler_params=pltpu.CompilerParams(vmem_limit_bytes=VMEM_BYTES), name="place_tokens",
        )(pltpu.with_memory_space_constraint(pieces, pltpu.HBM))
    return frame_map, token_map, mass_ratio


def solution(mesh):
    return jax.shard_map(
        shards,
        mesh=mesh,
        in_specs=(P("ctx", None), P("tok", None), P("ctx"), P("tok")),
        out_specs=(P("ctx", None), P("tok", None), P("ctx")),
        check_vma=False,
    )
```
